256 devices in a mesh: dp: 16 (over y, x), fsdp: 16 (over z, core).
Axes of the slice: x: 4, y: 4, z: 8, core: 2. Of those that a mesh axis runs over, the one named last changes fastest.
Arguments:
- fbank: bfloat16 [16, 16, 300, 640], P('dp', 'fsdp')
- lengths: int32 [16, 16, 3], replicated, may hold values from 50 to 200, as said below
- sources: int32 [16, 16, 3], replicated, may hold values from 0 to 47, as said below
- w_sub: bfloat16 [320, 1536], replicated, may hold values from -0.3125 to 0.3125
- gain_in: float32 [1536], replicated, may hold values from 0.25 to 1.75
- w_first: bfloat16 [1536, 3072], P(None, 'fsdp'), may hold values from -0.15625 to 0.15625
- taps: float32 [31, 1536], replicated, may hold values from -1 to 1
- gain_mid: float32 [1536], replicated, may hold values from 0.25 to 1.75
- w_second: bfloat16 [1536, 1536], P('fsdp'), may hold values from -0.15625 to 0.15625
- cotangent: bfloat16 [16, 16, 384, 1536], P('dp', 'fsdp'), may hold values from -0.046875 to 0.046875
Outputs:
- block_out: bfloat16 [16, 16, 384, 1536], P('dp', 'fsdp')
- grad_second: float32 [1536, 1536], P('fsdp')
- grad_taps: float32 [31, 1536], replicated
- grad_gain: float32 [1536], replicated
The draws below stay inside these ranges and needn't reach their ends.
Inputs may be any that keep to these rules, and one draw needn't show every extreme that they name: Every length is even; the lengths of one owner (one row along the last dimension) add up to exactly 384, and one of them is exactly 200. `sources`: within each group (first index) the values are a permutation of 0 to 47: value // 3 is the loader (index along dp) whose shard holds the utterance, value % 3 its place there. The 3 utterances of one owner come from 3 different loaders, so no loader holds two utterances of one owner. A loader's utterances lie one after another in order of place from row 0 of its shard, each taking its length // 2 rows; the shard's other rows belong to no utterance.
All inputs are finite; a program needn't handle non-finite values.
Results may differ from the reference program's by a relative error of at most 0.029.
Values may be sent and summed in bfloat16 or wider, within the bound.
No kernel may reach another device: no remote copies, remote signals or barrier semaphores. Data moves between devices by JAX's collectives and lax.ppermute only.
A program may use at most 128 MiB of HBM per device.

```python
import math
import jax
import jax.numpy as jnp
from jax import lax

D = 1536
BINS = 80
KERNEL = 31
MAXLEN = 200
MINLEN = 50
ROWS = 384
UTT = 3
LOAD = 300
N_DP = 16
N_FSDP = 16


def draw_fbank(key, part):
    key = jax.random.fold_in(key, 37)
    first, second, third = jax.random.split(key, 3)
    shape = (N_DP, N_FSDP, LOAD, 8 * BINS)
    base = jax.random.normal(first, shape, jnp.float32)
    row_scale = jnp.exp(jax.random.uniform(second, (N_DP, N_FSDP, LOAD, 1), jnp.float32) * math.log(10.0))
    column_scale = jnp.exp(jax.random.uniform(third, (8 * BINS,), jnp.float32) * math.log(10.0))
    return (base * row_scale * column_scale * 0.05).astype(jnp.bfloat16)


def draw_lengths(key, part):
    key = jax.random.fold_in(key, 11)
    first, second = jax.random.split(key)
    longest = MAXLEN // 2
    shortest = MINLEN // 2
    extra = ROWS // 2 - longest - (UTT - 1) * shortest
    weights = jax.random.randint(first, (N_FSDP, N_DP, UTT - 1), 750, 1000)
    totals = jnp.sum(weights, axis=-1, keepdims=True)
    share = extra * weights // totals
    leftover = extra - jnp.sum(share, axis=-1)
    share = share.at[..., 0].add(leftover)
    others = shortest + share
    pairs = jnp.concatenate([jnp.full((N_FSDP, N_DP, 1), longest, jnp.int32), others.astype(jnp.int32)], axis=-1)
    turn = jax.random.randint(second, (N_FSDP, N_DP, 1), 0, UTT)
    index = (jnp.arange(UTT, dtype=jnp.int32)[None, None, :] + turn) % UTT
    pairs = jnp.take_along_axis(pairs, index, axis=-1)
    return (2 * pairs).astype(jnp.int32)


def draw_sources(key, part):
    key = jax.random.fold_in(key, 23)
    keys = jax.random.split(key, 3)
    count = N_DP
    base = jax.vmap(lambda single: jax.random.permutation(single, count))(jax.random.split(keys[0], N_FSDP))
    base = base.astype(jnp.int32)
    shifts = jax.vmap(lambda single: jax.random.permutation(single, count))(jax.random.split(keys[1], N_FSDP))
    shifts = shifts[:, :UTT].astype(jnp.int32)
    owner = jnp.arange(count, dtype=jnp.int32)[None, :, None]
    spot = (owner + shifts[:, None, :]) % count
    loader = jnp.take_along_axis(base, spot.reshape(N_FSDP, count * UTT), axis=1).reshape(N_FSDP, count, UTT)
    offset = jax.random.randint(keys[2], (N_FSDP, count), 0, UTT)
    moved = jnp.take_along_axis(offset, loader.reshape(N_FSDP, count * UTT), axis=1).reshape(N_FSDP, count, UTT)
    place = (jnp.arange(UTT, dtype=jnp.int32)[None, None, :] + moved) % UTT
    return (loader * UTT + place).astype(jnp.int32)


def block_scale(stream_key, extent, pieces, least, high):
    factor_of = 1.0
    for dim, shards_of in pieces:
        heights = jax.random.uniform(jax.random.fold_in(jax.random.fold_in(stream_key, 6), dim), (shards_of,), jnp.float32, least / len(pieces), high / len(pieces))
        factor_of = factor_of * jnp.repeat(jnp.exp(heights), extent[dim] // shards_of).reshape((-1,) + (1,) * (len(extent) - 1 - dim))
    return factor_of


def noise(own_key, extent, scale, limit, shards=(), held_as=jnp.bfloat16):
    entries = jax.random.normal(own_key, extent, jnp.float32) * scale
    if len(shards) > 0:
        entries = block_scale(own_key, extent, shards, -0.22, 0.18) * entries
    return jnp.clip(entries, min=-limit, max=limit).astype(held_as)


def setup_inputs(seed: int = 0) -> dict:
    arg_keys = jax.random.split(jax.random.key(seed), 11)
    return {
        "fbank": draw_fbank(jax.random.fold_in(arg_keys[10], 71), 0),
        "lengths": draw_lengths(jax.random.fold_in(arg_keys[10], 71), 0),
        "sources": draw_sources(jax.random.fold_in(arg_keys[10], 71), 0),
        "w_sub": noise(arg_keys[3], (4 * BINS, D), (4 * BINS) ** -0.5, 0.3125),
        "gain_in": jnp.clip(1.0 + 0.15 * jax.random.normal(arg_keys[4], (D,), jnp.float32), 0.25, 1.75),
        "w_first": noise(arg_keys[5], (D, 2 * D), D ** -0.5, 0.15625, ((1, 16),)),
        "taps": noise(arg_keys[6], (KERNEL, D), KERNEL ** -0.5, 1.0, (), jnp.float32),
        "gain_mid": jnp.clip(1.0 + 0.15 * jax.random.normal(arg_keys[7], (D,), jnp.float32), 0.25, 1.75),
        "w_second": noise(arg_keys[8], (D, D), D ** -0.5, 0.15625, ((0, 16),)),
        "cotangent": noise(arg_keys[9], (N_DP, N_FSDP, ROWS, D), ((ROWS * N_DP * N_FSDP) ** -0.5), 0.046875, ((0, 16), (1, 16))),
    }


def plan_rows(lengths_group, sources_group, load, rows_half):
    utt = lengths_group.shape[-1]
    pairs = (lengths_group // 2).astype(jnp.int32)
    flat_pairs = pairs.reshape(-1)
    flat_source = sources_group.reshape(-1)
    loader = flat_source // utt
    place = flat_source % utt
    earlier = (loader[None, :] == loader[:, None]) & (place[None, :] < place[:, None])
    offset = lax.optimization_barrier(jnp.sum(jnp.where(earlier, flat_pairs[None, :], 0), axis=1)).astype(jnp.int32)
    begin = (loader * load + offset).astype(jnp.int32).reshape(pairs.shape)
    ends = jnp.cumsum(pairs, axis=1).astype(jnp.int32)
    starts = ends - pairs
    position = jnp.arange(rows_half, dtype=jnp.int32)
    inside = (position[None, None, :] >= starts[:, :, None]) & (position[None, None, :] < ends[:, :, None])
    source_row = lax.optimization_barrier(jnp.sum(jnp.where(inside, begin[:, :, None] + position[None, None, :] - starts[:, :, None], 0), axis=1))
    member = lax.optimization_barrier(jnp.sum(jnp.where(inside, jnp.arange(utt, dtype=jnp.int32)[None, :, None], 0), axis=1))
    return (source_row.astype(jnp.int32), member.astype(jnp.int32))

def layer_norm(values):
    mean = lax.optimization_barrier(jnp.mean(values, axis=-1, keepdims=True))
    spread = lax.optimization_barrier(jnp.mean(jnp.square(values - mean), axis=-1, keepdims=True))
    rstd = lax.rsqrt(spread + 1e-05)
    return ((values - mean) * rstd, rstd)

def shifted(values, offset, half):
    total = values.shape[0]
    padded = jnp.pad(values, ((half, half), (0, 0)))
    return padded[half + offset:half + offset + total]

def same_mask(member, offset, half):
    total = member.shape[0]
    padded = jnp.pad(member, (half, half), constant_values=-1)
    return (padded[half + offset:half + offset + total] == member)[:, None]

def front(pairs, w_sub, gain_in):
    frames = pairs.reshape(-1, w_sub.shape[0])
    first = jnp.dot(frames, w_sub, preferred_element_type=jnp.float32).astype(jnp.bfloat16)
    centered, rstd = layer_norm(first.astype(jnp.float32))
    return (first, (centered * gain_in).astype(jnp.bfloat16))

def middle(hidden, taps, gain_mid, member):
    width = hidden.shape[1] // 2
    glu = (hidden[:, :width] * jax.nn.sigmoid(hidden[:, width:])).astype(jnp.bfloat16)
    half = taps.shape[0] // 2
    conv = jnp.zeros((hidden.shape[0], width), jnp.float32)
    for tap in range(taps.shape[0]):
        offset = tap - half
        moved = jnp.where(same_mask(member, offset, half), shifted(glu, offset, half), 0)
        conv = conv + moved * taps[tap]
    centered, rstd = layer_norm(conv)
    normed = centered * gain_mid
    swished = (normed * jax.nn.sigmoid(normed)).astype(jnp.bfloat16)
    return (glu, centered, rstd, normed, swished)

def back(d_swished, normed, centered, rstd, gain_mid, glu, member, kernel):
    sig = jax.nn.sigmoid(normed)
    d_normed = d_swished * sig * (1.0 + normed * (1.0 - sig))
    gain_term = lax.optimization_barrier(jnp.sum(d_normed * centered, axis=0))
    scaled = d_normed * gain_mid
    d_conv = rstd * (scaled - lax.optimization_barrier(jnp.mean(scaled, axis=-1, keepdims=True)) - centered * lax.optimization_barrier(jnp.mean(scaled * centered, axis=-1, keepdims=True)))
    half = kernel // 2
    rows_out = []
    for tap in range(kernel):
        offset = tap - half
        moved = jnp.where(same_mask(member, offset, half), shifted(glu, offset, half), 0)
        rows_out.append(lax.optimization_barrier(jnp.sum(moved * d_conv, axis=0)))
    return (jnp.stack(rows_out, axis=0), gain_term)

def reference(fbank, lengths, sources, w_sub, gain_in, w_first, taps, gain_mid, w_second, cotangent):
    n_dp, n_fsdp, load, width = fbank.shape
    rows = cotangent.shape[2]
    kernel = taps.shape[0]

    def one(carry, index):
        owner = index // n_fsdp
        group = index % n_fsdp
        lengths_group = lax.dynamic_index_in_dim(lengths, group, 0, False)
        sources_group = lax.dynamic_index_in_dim(sources, group, 0, False)
        source_row, member_half = plan_rows(lengths_group, sources_group, load, rows // 2)
        loaders = lax.dynamic_index_in_dim(fbank, group, 1, False).reshape(n_dp * load, width)
        mine = lax.dynamic_index_in_dim(source_row, owner, 0, False)
        pairs = jnp.take(loaders, mine, axis=0)
        member = jnp.repeat(lax.dynamic_index_in_dim(member_half, owner, 0, False), 2)
        first, norm_in = front(pairs, w_sub, gain_in)
        hidden = jnp.dot(norm_in, w_first, preferred_element_type=jnp.float32)
        glu, centered, rstd, normed, swished = middle(hidden, taps, gain_mid, member)
        projected = lax.dot_general(swished, w_second, (((1,), (1,)), ((), ())), preferred_element_type=jnp.float32)
        block = (first.astype(jnp.float32) + projected).astype(jnp.bfloat16)
        grad_out = lax.dynamic_index_in_dim(lax.dynamic_index_in_dim(cotangent, owner, 0, False), group, 0, False)
        d_swished = jnp.dot(grad_out, w_second, preferred_element_type=jnp.float32)
        kernel_term, gain_term = back(d_swished, normed, centered, rstd, gain_mid, glu, member, kernel)
        weight_term = lax.dot_general(grad_out, swished, (((0,), (0,)), ((), ())), preferred_element_type=jnp.float32)
        return ((carry[0] + weight_term, carry[1] + kernel_term, carry[2] + gain_term), block)
    model = w_second.shape[0]
    start = (jnp.zeros((model, model), jnp.float32), jnp.zeros((kernel, model), jnp.float32), jnp.zeros((model,), jnp.float32))
    totals, blocks = lax.scan(one, start, jnp.arange(n_dp * n_fsdp, dtype=jnp.int32))
    block_out = blocks.reshape(n_dp, n_fsdp, rows, model)
    return (block_out, totals[0], totals[1], totals[2])
```

```python
import jax
import jax.numpy as jnp
from jax import lax
from jax.experimental import pallas as pl
from jax.experimental.pallas import tpu as pltpu
from jax.sharding import PartitionSpec as P

EDGE = 16
LANES = 128
SUBLANES = 8
BLOCK = 256
CONTRACT_LAST = (((1,), (1,)), ((), ()))


def row_chunk(total):
    for size in (104, 96, 80, 64, 48, 32, 16, 8):
        if total % size == 0:
            return size
    return total


def windows(pad_ref, base, size, lanes, kernel):
    reach = EDGE - kernel // 2
    for phase in range(SUBLANES):
        taps = [tap for tap in range(kernel) if (tap + reach) % SUBLANES == phase]
        if not taps:
            continue
        last = (taps[-1] + reach) // SUBLANES * SUBLANES
        held = pad_ref[base + phase : base + phase + last + size, lanes]
        for tap in taps:
            start = (tap + reach) // SUBLANES * SUBLANES
            yield tap, held[start : start + size]


def fill_padded(pad_ref, values):
    rows, width = values.shape
    zeros = jnp.zeros((EDGE, width), jnp.float32)
    pad_ref[:EDGE] = zeros
    pad_ref[EDGE + rows :] = zeros
    pad_ref[EDGE : EDGE + rows] = values


def forward_kernel(
    norm_ref, value_ref, gate_ref, taps_ref, gain_ref, select_ref,
    glu_ref, centered_ref, rstd_ref, swished_ref, pad_ref, conv_ref, half_ref,
):
    step = pl.program_id(0)
    steps = conv_ref.shape[0]
    rows, width = glu_ref.shape
    kernel = taps_ref.shape[0]
    norm = norm_ref[...]
    value = lax.dot_general(norm, value_ref[...], CONTRACT_LAST, preferred_element_type=jnp.float32)
    gate = lax.dot_general(norm, gate_ref[...], CONTRACT_LAST, preferred_element_type=jnp.float32)
    glu = (value * jax.nn.sigmoid(gate)).astype(jnp.bfloat16)
    glu_ref[...] = glu
    fill_padded(pad_ref, glu.astype(jnp.float32))
    size = row_chunk(rows)
    for column in range(0, width, LANES):
        lanes = slice(column, column + LANES)
        for base in range(0, rows, size):
            total = jnp.zeros((size, LANES), jnp.float32)
            for tap, moved in windows(pad_ref, base, size, lanes, kernel):
                total = total + moved * taps_ref[tap : tap + 1, lanes]
            conv_ref[step, base : base + size, lanes] = total

    @pl.when(step == steps - 1)
    def _():
        model = steps * width
        depth = 2 * SUBLANES

        def normalise(index, carry):
            chunk = pl.ds(pl.multiple_of(index * depth, depth), depth)
            parts = [conv_ref[block, chunk, :] for block in range(steps)]
            mean = sum(jnp.sum(part, axis=1, keepdims=True) for part in parts) / model
            parts = [part - mean for part in parts]
            spread = sum(jnp.sum(part * part, axis=1, keepdims=True) for part in parts) / model
            rstd = lax.rsqrt(spread + 1e-05)
            rstd_ref[chunk, :] = jnp.broadcast_to(rstd, (depth, LANES))
            for block in range(steps):
                centered = parts[block] * rstd
                centered_ref[block, chunk, :] = centered
                normed = centered * gain_ref[:, block * width : (block + 1) * width]
                half_ref[block, chunk, :] = (normed * jax.nn.sigmoid(normed)).astype(jnp.bfloat16)
            return carry

        lax.fori_loop(0, rows // depth, normalise, 0)
        for block in range(steps):
            swished_ref[:, block * width : (block + 1) * width] = jnp.dot(
                select_ref[...], half_ref[block], preferred_element_type=jnp.float32
            ).astype(jnp.bfloat16)


def forward(norm_in, first_t, taps, gain_mid, select):
    rows, model = norm_in.shape
    kernel = taps.shape[0]
    steps = model // BLOCK
    dense = select.shape[0]
    whole = lambda step: (0, 0)
    return pl.pallas_call(
        forward_kernel,
        grid=(steps,),
        in_specs=[
            pl.BlockSpec((rows, model), whole),
            pl.BlockSpec((BLOCK, model), lambda step: (step, 0)),
            pl.BlockSpec((BLOCK, model), lambda step: (step + steps, 0)),
            pl.BlockSpec((kernel, BLOCK), lambda step: (0, step)),
            pl.BlockSpec((1, model), whole),
            pl.BlockSpec((dense, rows), whole),
        ],
        out_specs=[
            pl.BlockSpec((rows, BLOCK), lambda step: (0, step)),
            pl.BlockSpec((steps, rows, BLOCK), lambda step: (0, 0, 0)),
            pl.BlockSpec((rows, LANES), whole),
            pl.BlockSpec((dense, model), whole),
        ],
        out_shape=[
            jax.ShapeDtypeStruct((rows, model), jnp.bfloat16),
            jax.ShapeDtypeStruct((steps, rows, BLOCK), jnp.float32),
            jax.ShapeDtypeStruct((rows, LANES), jnp.float32),
            jax.ShapeDtypeStruct((dense, model), jnp.bfloat16),
        ],
        scratch_shapes=[
            pltpu.VMEM((rows + 2 * EDGE, BLOCK), jnp.float32),
            pltpu.VMEM((steps, rows, BLOCK), jnp.float32),
            pltpu.VMEM((steps, rows, BLOCK), jnp.bfloat16),
        ],
        compiler_params=pltpu.CompilerParams(vmem_limit_bytes=48 * 2**20),
        cost_estimate=pl.CostEstimate(
            flops=4 * rows * model * model + 2 * kernel * rows * model,
            bytes_accessed=4 * model * model + 10 * rows * model,
            transcendentals=2 * rows * model,
        ),
        name="forward",
    )(norm_in, first_t, first_t, taps, gain_mid.reshape(1, model), select)


def backward_kernel(
    cotangent_ref, second_ref, centered_ref, rstd_ref, gain_ref, glu_ref,
    taps_out_ref, gain_out_ref, scaled_ref, sums_ref, pad_ref, part_ref,
):
    step = pl.program_id(0)
    steps = scaled_ref.shape[0]
    rows, width = glu_ref.shape
    kernel = taps_out_ref.shape[0]
    model = steps * width

    @pl.when(step == 0)
    def _():
        sums_ref[...] = jnp.zeros_like(sums_ref)

    @pl.when(step < steps)
    def _():
        scaled_ref[step] = jnp.dot(
            cotangent_ref[...], second_ref[...], preferred_element_type=jnp.float32
        )
        gain = gain_ref[...]
        depth = 32 if rows % 32 == 0 else SUBLANES

        def chunk_step(index, total):
            chunk = pl.ds(pl.multiple_of(index * depth, depth), depth)
            centered = centered_ref[0, chunk, :]
            normed = centered * gain
            sig = jax.nn.sigmoid(normed)
            d_normed = scaled_ref[step, chunk, :] * (sig * (1.0 + normed * (1.0 - sig)))
            weighed = d_normed * centered
            scaled = d_normed * gain
            scaled_ref[step, chunk, :] = scaled
            both = scaled * centered
            first = sums_ref[0, chunk, :]
            second = sums_ref[1, chunk, :]
            for column in range(0, width, LANES):
                first = first + scaled[:, column : column + LANES]
                second = second + both[:, column : column + LANES]
            sums_ref[0, chunk, :] = first
            sums_ref[1, chunk, :] = second
            return total + jnp.sum(weighed.reshape(-1, SUBLANES, width), axis=0)

        total = lax.fori_loop(
            0, rows // depth, chunk_step, jnp.zeros((SUBLANES, width), jnp.float32)
        )
        gain_out_ref[...] = jnp.sum(total, axis=0, keepdims=True)

    @pl.when(step == steps)
    def _():
        for index in range(2):
            mean = jnp.sum(sums_ref[index], axis=1, keepdims=True) / model
            sums_ref[index] = jnp.broadcast_to(mean, (rows, LANES))

    @pl.when(step >= steps)
    def _():
        block = step - steps
        fill_padded(pad_ref, glu_ref[...].astype(jnp.float32))
        size = row_chunk(rows)
        for column in range(0, width, LANES):
            lanes = slice(column, column + LANES)
            for base in range(0, rows, size):
                chunk = slice(base, base + size)
                d_conv = rstd_ref[chunk, :] * (
                    scaled_ref[block, chunk, lanes]
                    - sums_ref[0, chunk, :]
                    - centered_ref[0, chunk, lanes] * sums_ref[1, chunk, :]
                )
                for tap, moved in windows(pad_ref, base, size, lanes, kernel):
                    term = jnp.sum((moved * d_conv).reshape(-1, SUBLANES, LANES), axis=0)
                    if base == 0:
                        part_ref[tap, :, lanes] = term
                    else:
                        part_ref[tap, :, lanes] += term
        taps_out_ref[...] = jnp.sum(part_ref[...], axis=1)


def backward(cotangent, second, centered, rstd, gain_mid, glu, kernel):
    rows, model = cotangent.shape
    steps = model // BLOCK
    whole = lambda step: (0, 0)
    early = lambda step: (0, jnp.minimum(step, steps - 1))
    late = lambda step: (0, jnp.maximum(step - steps, 0))
    return pl.pallas_call(
        backward_kernel,
        grid=(2 * steps,),
        in_specs=[
            pl.BlockSpec((rows, model), whole),
            pl.BlockSpec((model, BLOCK), early),
            pl.BlockSpec((1, rows, BLOCK), lambda step: (step % steps, 0, 0)),
            pl.BlockSpec((rows, LANES), whole),
            pl.BlockSpec((1, BLOCK), early),
            pl.BlockSpec((rows, BLOCK), late),
        ],
        out_specs=[
            pl.BlockSpec((kernel, BLOCK), late),
            pl.BlockSpec((1, BLOCK), early),
        ],
        out_shape=[
            jax.ShapeDtypeStruct((kernel, model), jnp.float32),
            jax.ShapeDtypeStruct((1, model), jnp.float32),
        ],
        scratch_shapes=[
            pltpu.VMEM((steps, rows, BLOCK), jnp.float32),
            pltpu.VMEM((2, rows, LANES), jnp.float32),
            pltpu.VMEM((rows + 2 * EDGE, BLOCK), jnp.float32),
            pltpu.VMEM((kernel, SUBLANES, BLOCK), jnp.float32),
        ],
        compiler_params=pltpu.CompilerParams(vmem_limit_bytes=48 * 2**20),
        cost_estimate=pl.CostEstimate(
            flops=2 * rows * model * model + 2 * kernel * rows * model,
            bytes_accessed=2 * model * model + 12 * rows * model,
            transcendentals=rows * model,
        ),
        name="backward",
    )(cotangent, second, centered, rstd, gain_mid.reshape(1, model), glu)


def at(array, index, axis=0):
    return lax.dynamic_index_in_dim(array, index, axis, False)


def send_rows(fbank, lengths, sources, owner, utt, owners, most):
    halves = lengths.reshape(-1) // 2
    flat = sources.reshape(-1)
    places = jnp.arange(utt, dtype=jnp.int32) + owner * utt
    held = flat[None, :] == places[:, None]
    index = jnp.sum(jnp.where(held, jnp.arange(flat.shape[0], dtype=jnp.int32)[None, :], 0), axis=1)
    length = jnp.sum(jnp.where(held, halves[None, :], 0), axis=1)
    begin = jnp.cumsum(length) - length
    padded = jnp.pad(fbank, ((0, most), (0, 0)))
    blocks = jnp.zeros((owners, most, fbank.shape[1]), fbank.dtype)
    for place in range(utt):
        block = lax.dynamic_slice_in_dim(padded, begin[place], most, 0)
        blocks = lax.dynamic_update_index_in_dim(blocks, block, lax.div(index[place], utt), 0)
    return blocks


def place_rows(received, lengths, sources, rows_half):
    utt = lengths.shape[0]
    most = received.shape[1]
    halves = lengths // 2
    gap = EDGE // 2
    position = jnp.arange(rows_half + gap * (utt - 1), dtype=jnp.int32)
    column = jnp.full_like(position, -1)
    start = jnp.int32(0)
    for k in range(utt):
        inside = (position >= start) & (position < start + halves[k])
        column = jnp.where(inside, k * most + position - start, column)
        start = start + halves[k] + gap
    blocks = jnp.concatenate([at(received, lax.div(sources[k], utt)) for k in range(utt)], axis=0)
    return pick(one_hot(column, utt * most), blocks)


def frame_positions(lengths, rows):
    ends = jnp.cumsum(lengths)
    frame = jnp.arange(rows, dtype=jnp.int32)
    for k in range(lengths.shape[0] - 1):
        frame = frame + jnp.where(jnp.arange(rows, dtype=jnp.int32) >= ends[k], EDGE, 0)
    return frame


def one_hot(columns, count):
    wanted = jnp.arange(count, dtype=jnp.int32)
    return (columns[:, None] == wanted[None, :]).astype(jnp.bfloat16)


def layer_norm(values):
    mean = jnp.mean(values, axis=-1, keepdims=True)
    spread = jnp.mean(jnp.square(values - mean), axis=-1, keepdims=True)
    return (values - mean) * lax.rsqrt(spread + 1e-05)


def pick(matrix, values):
    return jnp.dot(matrix, values, preferred_element_type=jnp.float32).astype(jnp.bfloat16)


def spread(values, axis):
    copies = jnp.broadcast_to(values[None], (lax.axis_size(axis),) + values.shape)
    return lax.all_to_all(copies, axis, 0, 0, tiled=True)


def body(fbank, lengths, sources, w_sub, gain_in, w_first, taps, gain_mid, w_second, cotangent):
    owners = lax.axis_size("dp")
    groups = lax.axis_size("fsdp")
    chips = groups // 2
    owner = lax.axis_index("dp")
    group = lax.axis_index("fsdp")
    core = group % 2
    swap = [(i, i ^ 1) for i in range(groups)]
    same_core = [[2 * chip + side for chip in range(chips)] for side in range(2)]
    load, width = fbank.shape[2:]
    rows, model = cotangent.shape[2:]
    kernel = taps.shape[0]
    utt = lengths.shape[2]
    own_rows = w_second.shape[0]
    most = -(-(200 // 2) // SUBLANES) * SUBLANES

    first_t = lax.all_gather(w_first.T, "fsdp", axis=0, tiled=True)
    second = lax.all_gather(w_second, "fsdp", axis=0, tiled=True)

    lengths_group = at(lengths, group)
    sources_group = at(sources, group)
    own_lengths = at(lengths_group, owner)
    own_sources = at(sources_group, owner)
    blocks = send_rows(fbank.reshape(load, width), lengths_group, sources_group, owner, utt, owners, most)
    received = lax.all_to_all(blocks, "dp", 0, 0, tiled=True)
    pairs = place_rows(received, own_lengths, own_sources, rows // 2)
    frames = pairs.reshape(-1, w_sub.shape[0])
    spaced = frames.shape[0]
    select = one_hot(frame_positions(own_lengths, rows), spaced)

    x0 = jnp.dot(frames, w_sub, preferred_element_type=jnp.float32).astype(jnp.bfloat16)
    norm_in = (layer_norm(x0.astype(jnp.float32)) * gain_in).astype(jnp.bfloat16)
    x0 = pick(select, x0)
    grad_out = cotangent.reshape(rows, model)
    grad_spaced = pick(select.T, grad_out)
    grad_t = grad_out.T.reshape(chips, 2, own_rows, rows)
    grad_mine = at(grad_t, core, 1).reshape(chips * own_rows, rows)
    grad_theirs = lax.ppermute(
        at(grad_t, 1 - core, 1).reshape(chips * own_rows, rows), "fsdp", swap
    )

    norm_in, grad_spaced, grad_theirs = lax.optimization_barrier((norm_in, grad_spaced, grad_theirs))
    glu, centered, rstd, swished = forward(norm_in, first_t, taps, gain_mid, select)

    swished_theirs = lax.ppermute(swished, "fsdp", swap)
    partial = jnp.dot(
        jnp.concatenate([grad_mine, grad_theirs], axis=1),
        jnp.concatenate([swished, swished_theirs], axis=0),
        preferred_element_type=jnp.float32,
    ).astype(jnp.bfloat16)
    share = lax.psum_scatter(
        partial, "fsdp", scatter_dimension=0, tiled=True, axis_index_groups=same_core
    )

    taps_term, gain_term = backward(grad_spaced, second, centered, rstd, gain_mid, glu, kernel)
    projected = lax.dot_general(
        swished, second, CONTRACT_LAST, preferred_element_type=jnp.float32
    )
    block = (x0.astype(jnp.float32) + projected).astype(jnp.bfloat16)

    small = jnp.concatenate([taps_term, gain_term], axis=0).reshape(groups, -1, model)
    small = lax.all_to_all(small, "fsdp", 0, 0, tiled=True)
    small = spread(jnp.sum(small, axis=0).astype(jnp.bfloat16), "fsdp")

    own = own_rows // owners
    both = jnp.concatenate([share.reshape(owners, own, model), small.reshape(owners, -1, model)], axis=1)
    both = lax.all_to_all(both, "dp", 0, 0, tiled=True)
    both = spread(jnp.sum(both.astype(jnp.float32), axis=0).astype(jnp.bfloat16), "dp")
    both = both.astype(jnp.float32)
    grad_second = both[:, :own].reshape(own_rows, model)
    small = both[:, own:].reshape(kernel + 1, model)
    return (block.reshape(1, 1, rows, model), grad_second, small[:kernel], small[kernel])


def solution(mesh):
    in_specs = (
        P("dp", "fsdp", None, None),
        P(),
        P(),
        P(),
        P(),
        P(None, "fsdp"),
        P(),
        P(),
        P("fsdp", None),
        P("dp", "fsdp", None, None),
    )
    out_specs = (P("dp", "fsdp", None, None), P("fsdp", None), P(), P())
    return jax.shard_map(body, mesh=mesh, in_specs=in_specs, out_specs=out_specs, check_vma=False)
```

```python
import jax
import jax.numpy as jnp
from jax import lax
from jax.experimental import pallas as pl
from jax.experimental.pallas import tpu as pltpu
from jax.sharding import PartitionSpec as P

EDGE = 16
LANES = 128
SUBLANES = 8
FORWARD_STEPS = 6
BACKWARD_STEPS = 2
MOST = 104
CONTRACT_LAST = (((1,), (1,)), ((), ()))


def row_chunk(total):
    for size in (104, 96, 80, 64, 48, 32, 16, 8):
        if total % size == 0:
            return size
    return total


def windows(pad_ref, base, size, kernel):
    reach = EDGE - kernel // 2
    for phase in range(SUBLANES):
        taps = [tap for tap in range(kernel) if (tap + reach) % SUBLANES == phase]
        if not taps:
            continue
        last = (taps[-1] + reach) // SUBLANES * SUBLANES
        held = pad_ref[base + phase : base + phase + last + size, :]
        for tap in taps:
            start = (tap + reach) // SUBLANES * SUBLANES
            yield tap, held[start : start + size]


def fill_padded(pad_ref, values):
    rows, width = values.shape
    zeros = jnp.zeros((EDGE, LANES), jnp.float32)
    for index in range(width // LANES):
        pad_ref[index, :EDGE] = zeros
        pad_ref[index, EDGE + rows :] = zeros
        pad_ref[index, EDGE : EDGE + rows] = values[:, index * LANES : (index + 1) * LANES]


def sigmoid(values):
    return 0.5 * jnp.tanh(0.5 * values) + 0.5


def dot(left, right):
    return jnp.dot(left, right, preferred_element_type=jnp.float32)


def dot_t(left, right):
    return lax.dot_general(left, right, CONTRACT_LAST, preferred_element_type=jnp.float32)


def iotas(shape):
    return lax.broadcasted_iota(jnp.int32, shape, 0), lax.broadcasted_iota(jnp.int32, shape, 1)


def vmem(count):
    return [pl.BlockSpec(memory_space=pltpu.VMEM)] * count


def send_kernel(utt, owners, meta_ref, fbank_ref, blocks_ref):
    count = utt * owners
    owner = meta_ref[2 * count]
    dest = [jnp.int32(0)] * utt
    length = [jnp.int32(0)] * utt
    for index in range(count):
        place = meta_ref[count + index] - owner * utt
        half = lax.shift_right_logical(meta_ref[index], 1)
        for j in range(utt):
            hit = place == j
            dest[j] = jnp.where(hit, index // utt, dest[j])
            length[j] = jnp.where(hit, half, length[j])
    row, column = iotas((MOST, fbank_ref.shape[0]))
    begin = jnp.int32(0)
    for j in range(utt):
        chosen = (column == row + begin).astype(jnp.bfloat16)
        blocks_ref[dest[j]] = dot(chosen, fbank_ref[...]).astype(jnp.bfloat16)
        begin = begin + length[j]


def send_rows(meta, fbank, utt, owners):
    return pl.pallas_call(
        lambda *refs: send_kernel(utt, owners, *refs),
        in_specs=[pl.BlockSpec(memory_space=pltpu.SMEM)] + vmem(1),
        out_specs=vmem(1)[0],
        out_shape=jax.ShapeDtypeStruct((owners, MOST, fbank.shape[1]), jnp.bfloat16),
        compiler_params=pltpu.CompilerParams(vmem_limit_bytes=12 * 2**20),
        cost_estimate=pl.CostEstimate(flops=2 * 3 * MOST * 300 * 640, bytes_accessed=2 * 2**20, transcendentals=0),
        name="send_rows",
    )(meta, fbank)


def front_kernel(
    utt, owners, meta_ref, received_ref, sub_ref, gain_ref, cotangent_ref,
    norm_ref, dense_ref, select_ref, spaced_ref, wide_ref,
):
    count = utt * owners
    owner = meta_ref[2 * count]
    spaced, model = norm_ref.shape
    rows = dense_ref.shape[0]
    gap = EDGE // 2
    halves = [lax.shift_right_logical(meta_ref[owner * utt + k], 1) for k in range(utt)]
    row, column = iotas((spaced // 2, MOST))
    start = jnp.int32(0)
    pairs = jnp.zeros((spaced // 2, received_ref.shape[2]), jnp.float32)
    for k in range(utt):
        chosen = ((row == column + start) & (column < halves[k])).astype(jnp.bfloat16)
        loader = lax.div(meta_ref[count + owner * utt + k], jnp.int32(utt))
        pairs = pairs + dot(chosen, received_ref[loader])
        start = start + halves[k] + gap
    values = sub_ref.shape[0]
    even = dot(pairs[:, :values].astype(jnp.bfloat16), sub_ref[...]).astype(jnp.bfloat16)
    odd = dot(pairs[:, values:].astype(jnp.bfloat16), sub_ref[...]).astype(jnp.bfloat16)

    row, column = iotas((spaced, spaced // 2))
    wide_ref[...] = dot((row == 2 * column).astype(jnp.bfloat16), even) + dot(
        (row == 2 * column + 1).astype(jnp.bfloat16), odd
    )
    depth = 4 * SUBLANES if spaced % (4 * SUBLANES) == 0 else 2 * SUBLANES

    def normalise(index, carry):
        chunk = pl.ds(pl.multiple_of(index * depth, depth), depth)
        values = wide_ref[chunk, :]
        mean = jnp.sum(values, axis=1, keepdims=True) / model
        values = values - mean
        spread = jnp.sum(values * values, axis=1, keepdims=True) / model
        norm_ref[chunk, :] = (values * lax.rsqrt(spread + 1e-05) * gain_ref[...]).astype(jnp.bfloat16)
        return carry

    lax.fori_loop(0, spaced // depth, normalise, 0)

    def spread_out(frame):
        end = jnp.int32(0)
        moved = frame
        for k in range(utt - 1):
            end = end + 2 * halves[k]
            moved = moved + jnp.where(frame >= end, EDGE, 0)
        return moved

    frame, column = iotas((rows, spaced // 2))
    moved = spread_out(frame)
    dense_ref[...] = (
        dot((moved == 2 * column).astype(jnp.bfloat16), even)
        + dot((moved == 2 * column + 1).astype(jnp.bfloat16), odd)
    ).astype(jnp.bfloat16)
    frame, column = iotas((rows, spaced))
    select_ref[...] = (spread_out(frame) == column).astype(jnp.bfloat16)
    row, frame = iotas((spaced, rows))
    back = (spread_out(frame) == row).astype(jnp.bfloat16)
    spaced_ref[...] = dot(back, cotangent_ref[...]).astype(jnp.bfloat16)


def front(meta, received, w_sub, gain_in, cotangent, utt, owners):
    rows, model = cotangent.shape
    spaced = rows + EDGE * (utt - 1)
    bf16 = lambda *shape: jax.ShapeDtypeStruct(shape, jnp.bfloat16)
    return pl.pallas_call(
        lambda *refs: front_kernel(utt, owners, *refs),
        in_specs=[pl.BlockSpec(memory_space=pltpu.SMEM)] + vmem(4),
        out_specs=vmem(4),
        out_shape=[
            bf16(spaced, model), bf16(rows, model), bf16(rows, spaced), bf16(spaced, model),
        ],
        scratch_shapes=[pltpu.VMEM((spaced, model), jnp.float32)],
        compiler_params=pltpu.CompilerParams(vmem_limit_bytes=32 * 2**20),
        cost_estimate=pl.CostEstimate(flops=4 * 10**9, bytes_accessed=16 * 2**20, transcendentals=0),
        name="front",
    )(meta, received, w_sub, gain_in.reshape(1, model), cotangent)


def forward_kernel(
    norm_ref, value_ref, gate_ref, taps_ref, gain_ref, select_ref,
    glu_ref, centered_ref, rstd_ref, swished_ref, pad_ref, conv_ref, half_ref,
):
    step = pl.program_id(0)
    steps = pl.num_programs(0)
    rows, width = glu_ref.shape
    count = conv_ref.shape[0]
    blocks = width // LANES
    kernel = taps_ref.shape[0]
    weights = jnp.concatenate([value_ref[...], gate_ref[...]], axis=0)
    hidden = dot_t(norm_ref[...], weights)
    glu = (hidden[:, :width] * sigmoid(hidden[:, width:])).astype(jnp.bfloat16)
    glu_ref[...] = glu
    fill_padded(pad_ref, glu.astype(jnp.float32))
    size = row_chunk(rows)
    for index in range(blocks):
        lanes = slice(index * LANES, (index + 1) * LANES)
        for base in range(0, rows, size):
            total = jnp.zeros((size, LANES), jnp.float32)
            for tap, moved in windows(pad_ref.at[index], base, size, kernel):
                total = total + moved * taps_ref[tap : tap + 1, lanes]
            conv_ref[step * blocks + index, base : base + size, :] = total

    @pl.when(step == steps - 1)
    def _():
        model = count * LANES
        depth = 4 * SUBLANES if rows % (4 * SUBLANES) == 0 else 2 * SUBLANES

        def normalise(index, carry):
            chunk = pl.ds(pl.multiple_of(index * depth, depth), depth)
            parts = [conv_ref[block, chunk, :] for block in range(count)]
            mean = jnp.sum(sum(parts), axis=1, keepdims=True) / model
            parts = [part - mean for part in parts]
            spread = jnp.sum(sum(part * part for part in parts), axis=1, keepdims=True) / model
            rstd = lax.rsqrt(spread + 1e-05)
            rstd_ref[chunk, :] = jnp.broadcast_to(rstd, (depth, LANES))
            for block in range(count):
                centered = parts[block] * rstd
                centered_ref[block, chunk, :] = centered
                normed = centered * gain_ref[:, block * LANES : (block + 1) * LANES]
                half_ref[block // blocks, chunk, block % blocks * LANES : (block % blocks + 1) * LANES] = (
                    normed * sigmoid(normed)
                ).astype(jnp.bfloat16)
            return carry

        lax.fori_loop(0, rows // depth, normalise, 0)
        for slot in range(count // blocks):
            swished_ref[:, slot * width : (slot + 1) * width] = dot(
                select_ref[...], half_ref[slot]
            ).astype(jnp.bfloat16)


def forward(norm_in, first_t, taps, gain_mid, select):
    rows, model = norm_in.shape
    kernel = taps.shape[0]
    steps = FORWARD_STEPS
    width = model // steps
    dense = select.shape[0]
    whole = lambda step: (0, 0)
    return pl.pallas_call(
        forward_kernel,
        grid=(steps,),
        in_specs=[
            pl.BlockSpec((rows, model), whole),
            pl.BlockSpec((width, model), lambda step: (step, 0)),
            pl.BlockSpec((width, model), lambda step: (step + steps, 0)),
            pl.BlockSpec((kernel, width), lambda step: (0, step)),
            pl.BlockSpec((1, model), whole),
            pl.BlockSpec((dense, rows), whole),
        ],
        out_specs=[
            pl.BlockSpec((rows, width), lambda step: (0, step)),
            pl.BlockSpec((model // LANES, rows, LANES), lambda step: (0, 0, 0)),
            pl.BlockSpec((rows, LANES), whole),
            pl.BlockSpec((dense, model), whole),
        ],
        out_shape=[
            jax.ShapeDtypeStruct((rows, model), jnp.bfloat16),
            jax.ShapeDtypeStruct((model // LANES, rows, LANES), jnp.float32),
            jax.ShapeDtypeStruct((rows, LANES), jnp.float32),
            jax.ShapeDtypeStruct((dense, model), jnp.bfloat16),
        ],
        scratch_shapes=[
            pltpu.VMEM((width // LANES, rows + 2 * EDGE, LANES), jnp.float32),
            pltpu.VMEM((model // LANES, rows, LANES), jnp.float32),
            pltpu.VMEM((steps, rows, width), jnp.bfloat16),
        ],
        compiler_params=pltpu.CompilerParams(vmem_limit_bytes=50 * 2**20),
        cost_estimate=pl.CostEstimate(
            flops=4 * rows * model * model + 20 * kernel * rows * model,
            bytes_accessed=4 * model * model + 10 * rows * model,
            transcendentals=2 * rows * model,
        ),
        name="forward",
    )(norm_in, first_t, first_t, taps, gain_mid.reshape(1, model), select)


def backward_kernel(
    cotangent_ref, second_ref, slope_ref, centered_ref, rstd_ref, gain_ref, glu_ref,
    taps_out_ref, gain_out_ref, scaled_ref, sums_ref, pad_ref, part_ref,
):
    step = pl.program_id(0)
    steps = pl.num_programs(0) // 2
    rows, width = glu_ref.shape
    kernel = taps_out_ref.shape[0]
    blocks = width // LANES
    model = steps * width

    @pl.when(step == 0)
    def _():
        sums_ref[...] = jnp.zeros_like(sums_ref)

    @pl.when(step < steps)
    def _():
        d_swished = dot(cotangent_ref[...], second_ref[...])
        for index in range(blocks):
            scaled_ref[step * blocks + index] = d_swished[:, index * LANES : (index + 1) * LANES]
        depth = 4 * SUBLANES if rows % (4 * SUBLANES) == 0 else 2 * SUBLANES

        def chunk_step(number, totals):
            chunk = pl.ds(pl.multiple_of(number * depth, depth), depth)
            first = sums_ref[0, chunk, :]
            second = sums_ref[1, chunk, :]
            result = []
            for index in range(blocks):
                place = step * blocks + index
                scaled = scaled_ref[place, chunk, :] * slope_ref[index, chunk, :]
                scaled_ref[place, chunk, :] = scaled
                both = scaled * centered_ref[index, chunk, :]
                first = first + scaled
                second = second + both
                result.append(totals[index] + jnp.sum(both.reshape(-1, SUBLANES, LANES), axis=0))
            sums_ref[0, chunk, :] = first
            sums_ref[1, chunk, :] = second
            return tuple(result)

        zero = jnp.zeros((SUBLANES, LANES), jnp.float32)
        totals = lax.fori_loop(0, rows // depth, chunk_step, (zero,) * blocks)
        for index in range(blocks):
            lanes = slice(index * LANES, (index + 1) * LANES)
            gain_out_ref[:, lanes] = jnp.sum(totals[index], axis=0, keepdims=True) / gain_ref[:, lanes]

    @pl.when(step == steps)
    def _():
        for index in range(2):
            mean = jnp.sum(sums_ref[index], axis=1, keepdims=True) / model
            sums_ref[index] = jnp.broadcast_to(mean, (rows, LANES))

    @pl.when(step >= steps)
    def _():
        fill_padded(pad_ref, glu_ref[...].astype(jnp.float32))
        size = row_chunk(rows)
        for index in range(blocks):
            lanes = slice(index * LANES, (index + 1) * LANES)
            for base in range(0, rows, size):
                chunk = slice(base, base + size)
                d_conv = rstd_ref[chunk, :] * (
                    scaled_ref[(step - steps) * blocks + index, chunk, :]
                    - sums_ref[0, chunk, :]
                    - centered_ref[index, chunk, :] * sums_ref[1, chunk, :]
                )
                for tap, moved in windows(pad_ref.at[index], base, size, kernel):
                    term = jnp.sum((moved * d_conv).reshape(-1, SUBLANES, LANES), axis=0)
                    if base == 0:
                        part_ref[index, tap] = term
                    else:
                        part_ref[index, tap] += term
            taps_out_ref[:, lanes] = jnp.sum(part_ref[index], axis=1)


def backward(cotangent, second, slope, centered, rstd, gain_mid, glu, kernel):
    rows, model = cotangent.shape
    steps = BACKWARD_STEPS
    width = model // steps
    blocks = width // LANES
    whole = lambda step: (0, 0)
    early = lambda step: (0, jnp.minimum(step, steps - 1))
    late = lambda step: (0, jnp.maximum(step - steps, 0))
    return pl.pallas_call(
        backward_kernel,
        grid=(2 * steps,),
        in_specs=[
            pl.BlockSpec((rows, model), whole),
            pl.BlockSpec((model, width), early),
            pl.BlockSpec((blocks, rows, LANES), lambda step: (jnp.minimum(step, steps - 1), 0, 0)),
            pl.BlockSpec((blocks, rows, LANES), lambda step: (lax.rem(step, steps), 0, 0)),
            pl.BlockSpec((rows, LANES), whole),
            pl.BlockSpec((1, width), early),
            pl.BlockSpec((rows, width), late),
        ],
        out_specs=[pl.BlockSpec((kernel, width), late), pl.BlockSpec((1, width), early)],
        out_shape=[
            jax.ShapeDtypeStruct((kernel, model), jnp.float32),
            jax.ShapeDtypeStruct((1, model), jnp.float32),
        ],
        scratch_shapes=[
            pltpu.VMEM((model // LANES, rows, LANES), jnp.float32),
            pltpu.VMEM((2, rows, LANES), jnp.float32),
            pltpu.VMEM((blocks, rows + 2 * EDGE, LANES), jnp.float32),
            pltpu.VMEM((blocks, kernel, SUBLANES, LANES), jnp.float32),
        ],
        compiler_params=pltpu.CompilerParams(vmem_limit_bytes=54 * 2**20),
        cost_estimate=pl.CostEstimate(
            flops=2 * rows * model * model + 20 * kernel * rows * model,
            bytes_accessed=2 * model * model + 12 * rows * model,
            transcendentals=rows * model,
        ),
        name="backward",
    )(cotangent, second, slope, centered, rstd, gain_mid.reshape(1, model), glu)


def weight_kernel(mine_ref, theirs_ref, swished_ref, other_ref, out_ref):
    out_ref[...] = (dot(mine_ref[...], swished_ref[...]) + dot(theirs_ref[...], other_ref[...])).astype(jnp.bfloat16)


def weight_gradient(mine, theirs, swished, other):
    out, rows = mine.shape
    model = swished.shape[1]
    width = model // 3
    whole = pl.BlockSpec((out, rows), lambda step: (0, 0))
    block = pl.BlockSpec((rows, width), lambda step: (0, step))
    return pl.pallas_call(
        weight_kernel,
        grid=(model // width,),
        in_specs=[whole, whole, block, block],
        out_specs=pl.BlockSpec((out, width), lambda step: (0, step)),
        out_shape=jax.ShapeDtypeStruct((out, model), jnp.bfloat16),
        compiler_params=pltpu.CompilerParams(vmem_limit_bytes=16 * 2**20),
        cost_estimate=pl.CostEstimate(
            flops=4 * rows * out * model, bytes_accessed=2 * out * model, transcendentals=0
        ),
        name="weight_gradient",
    )(mine, theirs, swished, other)


def spread(values, axis):
    copies = jnp.broadcast_to(values[None], (lax.axis_size(axis),) + values.shape)
    return lax.all_to_all(copies, axis, 0, 0, tiled=True)


def at(array, index, axis=0):
    return lax.dynamic_index_in_dim(array, index, axis, False)


def barrier(values):
    return lax.optimization_barrier(values)


def scatter_plane(values, owner):
    owners = values.shape[0]
    side = 4 if owners % 4 == 0 else 1
    across, along = lax.rem(owner, side), lax.div(owner, side)
    values = values.reshape((owners // side, side) + values.shape[1:])
    total = at(values, across, 1)
    for k in range(1, side):
        moves = [(i, i // side * side + (i % side + k) % side) for i in range(owners)]
        total = total + lax.ppermute(at(values, lax.rem(across + k, side), 1), "dp", moves)
    values, count = total, owners // side
    total = at(values, along)
    for k in range(1, count):
        moves = [(i, (i // side + k) % count * side + i % side) for i in range(owners)]
        total = total + lax.ppermute(at(values, lax.rem(along + k, count)), "dp", moves)
    return total


def body(fbank, lengths, sources, w_sub, gain_in, w_first, taps, gain_mid, w_second, cotangent):
    owners = lax.axis_size("dp")
    groups = lax.axis_size("fsdp")
    chips = groups // 2
    owner = lax.axis_index("dp")
    group = lax.axis_index("fsdp")
    core = lax.rem(group, 2)
    load, width = fbank.shape[2:]
    rows, model = cotangent.shape[2:]
    kernel = taps.shape[0]
    utt = lengths.shape[2]
    own_rows = w_second.shape[0]
    own = own_rows // owners

    swap = lambda block: lax.ppermute(block, "fsdp", [(i, i ^ 1) for i in range(groups)])

    first_t = lax.all_gather(w_first.T, "fsdp", axis=0, tiled=True)
    second = lax.all_gather(w_second, "fsdp", axis=0, tiled=True)

    meta = jnp.concatenate(
        [at(lengths, group).reshape(-1), at(sources, group).reshape(-1), jnp.stack([owner, group])]
    )
    blocks = send_rows(meta, fbank.reshape(load, width), utt, owners)
    received = lax.all_to_all(blocks, "dp", 0, 0, tiled=True)

    grad_out = cotangent.reshape(rows, model)
    grad_t = grad_out.T.reshape(chips, 2, owners, own, rows)
    of_core = lambda side: jnp.swapaxes(at(grad_t, side, 1), 0, 1).reshape(chips * own_rows, rows)
    grad_mine, grad_theirs = of_core(core), swap(of_core(1 - core))

    norm_in, x0, select, grad_spaced = front(meta, received, w_sub, gain_in, grad_out, utt, owners)
    norm_in, grad_mine, grad_theirs = barrier((norm_in, grad_mine, grad_theirs))
    glu, centered, rstd, swished = forward(norm_in, first_t, taps, gain_mid, select)

    partial = weight_gradient(grad_mine, grad_theirs, swished, swap(swished))
    centered, partial = barrier((centered, partial))
    partial = lax.all_to_all(partial.reshape(owners, chips * own, model), "dp", 0, 0, tiled=True)

    gains = gain_mid.reshape(-1, 1, LANES)
    normed = centered * gains
    sig = sigmoid(normed)
    slope = gains * (sig * (1.0 + normed * (1.0 - sig)))
    taps_term, gain_term = backward(grad_spaced, second, slope, centered, rstd, gain_mid, glu, kernel)
    block = (x0.astype(jnp.float32) + dot_t(swished, second)).astype(jnp.bfloat16)

    small = jnp.concatenate([taps_term, gain_term], axis=0)
    small = scatter_plane(small.reshape(owners, -1, model), owner)
    partial = jnp.sum(partial.astype(jnp.float32), axis=0).astype(jnp.bfloat16).reshape(chips, own, model)

    small = (small + swap(small)).astype(jnp.bfloat16)
    both = jnp.concatenate([partial, jnp.broadcast_to(small[None], (chips,) + small.shape)], axis=1)
    same_core = [[2 * chip + side for chip in range(chips)] for side in range(2)]
    both = lax.all_to_all(both, "fsdp", 0, 0, tiled=True, axis_index_groups=same_core)
    both = jnp.sum(both.astype(jnp.float32), axis=0).astype(jnp.bfloat16)
    both = spread(both, "dp").astype(jnp.float32)
    grad_second = both[:, :own].reshape(own_rows, model)
    small = both[:, own:].reshape(kernel + 1, model)
    return (block.reshape(1, 1, rows, model), grad_second, small[:kernel], small[kernel])


def solution(mesh):
    in_specs = (
        P("dp", "fsdp", None, None),
        P(),
        P(),
        P(),
        P(),
        P(None, "fsdp"),
        P(),
        P(),
        P("fsdp", None),
        P("dp", "fsdp", None, None),
    )
    out_specs = (P("dp", "fsdp", None, None), P("fsdp", None), P(), P())
    return jax.shard_map(body, mesh=mesh, in_specs=in_specs, out_specs=out_specs, check_vma=False)
```

```python
import jax
import jax.numpy as jnp
from jax import lax
from jax.experimental import pallas as pl
from jax.experimental.pallas import tpu as pltpu
from jax.sharding import PartitionSpec as P

EDGE = 16
LANES = 128
SUBLANES = 8
FORWARD_STEPS = 6
BACKWARD_STEPS = 2
MOST = 104
CONTRACT_LAST = (((1,), (1,)), ((), ()))


def row_chunk(total):
    for size in (104, 96, 80, 64, 48, 32, 16, 8):
        if total % size == 0:
            return size
    return total


def windows(pad_ref, base, size, kernel):
    reach = EDGE - kernel // 2
    for phase in range(SUBLANES):
        taps = [tap for tap in range(kernel) if (tap + reach) % SUBLANES == phase]
        if not taps:
            continue
        last = (taps[-1] + reach) // SUBLANES * SUBLANES
        held = pad_ref[base + phase : base + phase + last + size, :]
        for tap in taps:
            start = (tap + reach) // SUBLANES * SUBLANES
            yield tap, held[start : start + size]


def fill_padded(pad_ref, values):
    rows, width = values.shape
    zeros = jnp.zeros((EDGE, LANES), jnp.float32)
    for index in range(width // LANES):
        pad_ref[index, :EDGE] = zeros
        pad_ref[index, EDGE + rows :] = zeros
        pad_ref[index, EDGE : EDGE + rows] = values[:, index * LANES : (index + 1) * LANES]


def sigmoid(values):
    return 0.5 * jnp.tanh(0.5 * values) + 0.5


def dot(left, right):
    return jnp.dot(left, right, preferred_element_type=jnp.float32)


def dot_t(left, right):
    return lax.dot_general(left, right, CONTRACT_LAST, preferred_element_type=jnp.float32)


def iotas(shape):
    return lax.broadcasted_iota(jnp.int32, shape, 0), lax.broadcasted_iota(jnp.int32, shape, 1)


def vmem(count):
    return [pl.BlockSpec(memory_space=pltpu.VMEM)] * count


def own_halves(meta_ref, utt, owners):
    owner = meta_ref[2 * utt * owners]
    return [lax.shift_right_logical(meta_ref[owner * utt + k], 1) for k in range(utt)]


def spaced_row(frame, halves):
    end = jnp.int32(0)
    moved = frame
    for half in halves[:-1]:
        end = end + 2 * half
        moved = moved + jnp.where(frame >= end, EDGE, 0)
    return moved


def send_kernel(utt, owners, meta_ref, fbank_ref, blocks_ref):
    count = utt * owners
    owner = meta_ref[2 * count]
    dest = [jnp.int32(0)] * utt
    length = [jnp.int32(0)] * utt
    for index in range(count):
        place = meta_ref[count + index] - owner * utt
        half = lax.shift_right_logical(meta_ref[index], 1)
        for j in range(utt):
            hit = place == j
            dest[j] = jnp.where(hit, index // utt, dest[j])
            length[j] = jnp.where(hit, half, length[j])
    row, column = iotas((MOST, fbank_ref.shape[0]))
    begin = jnp.int32(0)
    for j in range(utt):
        chosen = (column == row + begin).astype(jnp.bfloat16)
        blocks_ref[dest[j]] = dot(chosen, fbank_ref[...]).astype(jnp.bfloat16)
        begin = begin + length[j]


def send_rows(meta, fbank, utt, owners):
    return pl.pallas_call(
        lambda *refs: send_kernel(utt, owners, *refs),
        in_specs=[pl.BlockSpec(memory_space=pltpu.SMEM)] + vmem(1),
        out_specs=vmem(1)[0],
        out_shape=jax.ShapeDtypeStruct((owners, MOST, fbank.shape[1]), jnp.bfloat16),
        compiler_params=pltpu.CompilerParams(vmem_limit_bytes=12 * 2**20),
        cost_estimate=pl.CostEstimate(flops=2 * 3 * MOST * 300 * 640, bytes_accessed=2 * 2**20, transcendentals=0),
        name="send_rows",
    )(meta, fbank)


def front_kernel(
    utt, owners, meta_ref, received_ref, sub_ref, gain_ref, cotangent_ref,
    norm_ref, dense_ref, spaced_ref, wide_ref,
):
    count = utt * owners
    owner = meta_ref[2 * count]
    spaced, model = norm_ref.shape
    rows = dense_ref.shape[0]
    gap = EDGE // 2
    halves = own_halves(meta_ref, utt, owners)
    row, column = iotas((spaced // 2, MOST))
    start = jnp.int32(0)
    pairs = jnp.zeros((spaced // 2, received_ref.shape[2]), jnp.float32)
    for k in range(utt):
        chosen = ((row == column + start) & (column < halves[k])).astype(jnp.bfloat16)
        loader = lax.div(meta_ref[count + owner * utt + k], jnp.int32(utt))
        pairs = pairs + dot(chosen, received_ref[loader])
        start = start + halves[k] + gap
    values = sub_ref.shape[0]
    even = dot(pairs[:, :values].astype(jnp.bfloat16), sub_ref[...]).astype(jnp.bfloat16)
    odd = dot(pairs[:, values:].astype(jnp.bfloat16), sub_ref[...]).astype(jnp.bfloat16)

    row, column = iotas((spaced, spaced // 2))
    wide_ref[...] = dot((row == 2 * column).astype(jnp.bfloat16), even) + dot(
        (row == 2 * column + 1).astype(jnp.bfloat16), odd
    )
    depth = 4 * SUBLANES if spaced % (4 * SUBLANES) == 0 else 2 * SUBLANES

    def normalise(index, carry):
        chunk = pl.ds(pl.multiple_of(index * depth, depth), depth)
        values = wide_ref[chunk, :]
        mean = jnp.sum(values, axis=1, keepdims=True) / model
        values = values - mean
        spread = jnp.sum(values * values, axis=1, keepdims=True) / model
        norm_ref[chunk, :] = (values * lax.rsqrt(spread + 1e-05) * gain_ref[...]).astype(jnp.bfloat16)
        return carry

    lax.fori_loop(0, spaced // depth, normalise, 0)

    frame, column = iotas((rows, spaced // 2))
    moved = spaced_row(frame, halves)
    dense_ref[...] = (
        dot((moved == 2 * column).astype(jnp.bfloat16), even)
        + dot((moved == 2 * column + 1).astype(jnp.bfloat16), odd)
    ).astype(jnp.bfloat16)
    row, frame = iotas((spaced, rows))
    back = (spaced_row(frame, halves) == row).astype(jnp.bfloat16)
    spaced_ref[...] = dot(back, cotangent_ref[...]).astype(jnp.bfloat16)


def front(meta, received, w_sub, gain_in, cotangent, utt, owners):
    rows, model = cotangent.shape
    spaced = rows + EDGE * (utt - 1)
    bf16 = lambda *shape: jax.ShapeDtypeStruct(shape, jnp.bfloat16)
    return pl.pallas_call(
        lambda *refs: front_kernel(utt, owners, *refs),
        in_specs=[pl.BlockSpec(memory_space=pltpu.SMEM)] + vmem(4),
        out_specs=vmem(3),
        out_shape=[
            bf16(spaced, model), bf16(rows, model), bf16(spaced, model),
        ],
        scratch_shapes=[pltpu.VMEM((spaced, model), jnp.float32)],
        compiler_params=pltpu.CompilerParams(vmem_limit_bytes=32 * 2**20),
        cost_estimate=pl.CostEstimate(flops=4 * 10**9, bytes_accessed=16 * 2**20, transcendentals=0),
        name="front",
    )(meta, received, w_sub, gain_in.reshape(1, model), cotangent)


def forward_kernel(
    utt, owners, meta_ref, norm_ref, value_ref, gate_ref, taps_ref, gain_ref,
    glu_ref, conv_out_ref, mean_ref, rstd_ref, swished_ref, pad_ref, conv_ref, half_ref,
):
    step = pl.program_id(0)
    steps = pl.num_programs(0)
    rows, width = glu_ref.shape
    count = conv_ref.shape[0]
    blocks = width // LANES
    kernel = taps_ref.shape[0]
    @pl.when(step == 0)
    def _():
        mean_ref[...] = jnp.zeros_like(mean_ref)

    value = dot_t(norm_ref[...], value_ref[...])
    gate = dot_t(norm_ref[...], gate_ref[...])
    glu = (value * sigmoid(gate)).astype(jnp.bfloat16)
    glu_ref[...] = glu
    fill_padded(pad_ref, glu.astype(jnp.float32))
    size = row_chunk(rows)
    for index in range(blocks):
        lanes = slice(index * LANES, (index + 1) * LANES)
        for base in range(0, rows, size):
            total = jnp.zeros((size, LANES), jnp.float32)
            for tap, moved in windows(pad_ref.at[index], base, size, kernel):
                total = total + moved * taps_ref[tap : tap + 1, lanes]
            conv_ref[step * blocks + index, base : base + size, :] = total
            conv_out_ref[index, base : base + size, :] = total
            mean_ref[base : base + size, :] += total

    @pl.when(step == steps - 1)
    def _():
        model = count * LANES
        depth = 4 * SUBLANES if rows % (4 * SUBLANES) == 0 else 2 * SUBLANES

        def normalise(index, carry):
            chunk = pl.ds(pl.multiple_of(index * depth, depth), depth)
            parts = [conv_ref[block, chunk, :] for block in range(count)]
            mean = jnp.sum(mean_ref[chunk, :], axis=1, keepdims=True) / model
            mean_ref[chunk, :] = jnp.broadcast_to(mean, (depth, LANES))
            parts = [part - mean for part in parts]
            spread = jnp.sum(sum(part * part for part in parts), axis=1, keepdims=True) / model
            rstd = lax.rsqrt(spread + 1e-05)
            rstd_ref[chunk, :] = jnp.broadcast_to(rstd, (depth, LANES))
            for block in range(count):
                normed = parts[block] * rstd * gain_ref[:, block * LANES : (block + 1) * LANES]
                half_ref[block // blocks, chunk, block % blocks * LANES : (block % blocks + 1) * LANES] = (
                    normed * sigmoid(normed)
                ).astype(jnp.bfloat16)
            return carry

        lax.fori_loop(0, rows // depth, normalise, 0, unroll=True)
        frame, column = iotas((swished_ref.shape[0], rows))
        chosen = (spaced_row(frame, own_halves(meta_ref, utt, owners)) == column).astype(jnp.bfloat16)
        for slot in range(count // blocks):
            swished_ref[:, slot * width : (slot + 1) * width] = dot(chosen, half_ref[slot]).astype(jnp.bfloat16)


def forward(meta, norm_in, first_t, taps, gain_mid, dense, utt, owners):
    rows, model = norm_in.shape
    kernel = taps.shape[0]
    steps = FORWARD_STEPS
    width = model // steps
    whole = lambda step: (0, 0)
    return pl.pallas_call(
        lambda *refs: forward_kernel(utt, owners, *refs),
        grid=(steps,),
        in_specs=[
            pl.BlockSpec(memory_space=pltpu.SMEM),
            pl.BlockSpec((rows, model), whole),
            pl.BlockSpec((width, model), lambda step: (step, 0)),
            pl.BlockSpec((width, model), lambda step: (step + steps, 0)),
            pl.BlockSpec((kernel, width), lambda step: (0, step)),
            pl.BlockSpec((1, model), whole),
        ],
        out_specs=[
            pl.BlockSpec((rows, width), lambda step: (0, step)),
            pl.BlockSpec((width // LANES, rows, LANES), lambda step: (step, 0, 0)),
            pl.BlockSpec((rows, LANES), whole),
            pl.BlockSpec((rows, LANES), whole),
            pl.BlockSpec((dense, model), whole),
        ],
        out_shape=[
            jax.ShapeDtypeStruct((rows, model), jnp.bfloat16),
            jax.ShapeDtypeStruct((model // LANES, rows, LANES), jnp.float32),
            jax.ShapeDtypeStruct((rows, LANES), jnp.float32),
            jax.ShapeDtypeStruct((rows, LANES), jnp.float32),
            jax.ShapeDtypeStruct((dense, model), jnp.bfloat16),
        ],
        scratch_shapes=[
            pltpu.VMEM((width // LANES, rows + 2 * EDGE, LANES), jnp.float32),
            pltpu.VMEM((model // LANES, rows, LANES), jnp.float32),
            pltpu.VMEM((steps, rows, width), jnp.bfloat16),
        ],
        compiler_params=pltpu.CompilerParams(vmem_limit_bytes=50 * 2**20),
        cost_estimate=pl.CostEstimate(
            flops=4 * rows * model * model + 20 * kernel * rows * model,
            bytes_accessed=4 * model * model + 10 * rows * model,
            transcendentals=2 * rows * model,
        ),
        name="forward",
    )(meta, norm_in, first_t, first_t, taps, gain_mid.reshape(1, model))


def backward_kernel(
    cotangent_ref, second_ref, slope_ref, centered_ref, rstd_ref, gain_ref, glu_ref,
    small_ref, scaled_ref, sums_ref, pad_ref, part_ref,
):
    step = pl.program_id(0)
    steps = pl.num_programs(0) // 2
    rows, width = glu_ref.shape
    kernel = small_ref.shape[0] - 1
    blocks = width // LANES
    model = steps * width

    @pl.when(step == 0)
    def _():
        sums_ref[...] = jnp.zeros_like(sums_ref)

    @pl.when(step < steps)
    def _():
        d_swished = dot(cotangent_ref[...], second_ref[...])
        for index in range(blocks):
            scaled_ref[step * blocks + index] = d_swished[:, index * LANES : (index + 1) * LANES]
        depth = 4 * SUBLANES if rows % (4 * SUBLANES) == 0 else 2 * SUBLANES

        def chunk_step(number, totals):
            chunk = pl.ds(pl.multiple_of(number * depth, depth), depth)
            first = sums_ref[0, chunk, :]
            second = sums_ref[1, chunk, :]
            result = []
            for index in range(blocks):
                place = step * blocks + index
                scaled = scaled_ref[place, chunk, :] * slope_ref[index, chunk, :]
                scaled_ref[place, chunk, :] = scaled
                both = scaled * centered_ref[index, chunk, :]
                first = first + scaled
                second = second + both
                result.append(totals[index] + jnp.sum(both.reshape(-1, SUBLANES, LANES), axis=0))
            sums_ref[0, chunk, :] = first
            sums_ref[1, chunk, :] = second
            return tuple(result)

        zero = jnp.zeros((SUBLANES, LANES), jnp.float32)
        totals = lax.fori_loop(0, rows // depth, chunk_step, (zero,) * blocks)
        for index in range(blocks):
            lanes = slice(index * LANES, (index + 1) * LANES)
            place = pl.ds(pl.multiple_of((step * blocks + index) * LANES, LANES), LANES)
            small_ref[kernel:, place] = jnp.sum(totals[index], axis=0, keepdims=True) / gain_ref[:, lanes]

    @pl.when(step == steps)
    def _():
        for index in range(2):
            mean = jnp.sum(sums_ref[index], axis=1, keepdims=True) / model
            sums_ref[index] = jnp.broadcast_to(mean, (rows, LANES))

    @pl.when(step >= steps)
    def _():
        fill_padded(pad_ref, glu_ref[...].astype(jnp.float32))
        size = row_chunk(rows)
        for index in range(blocks):
            for base in range(0, rows, size):
                chunk = slice(base, base + size)
                d_conv = rstd_ref[chunk, :] * (
                    scaled_ref[(step - steps) * blocks + index, chunk, :]
                    - sums_ref[0, chunk, :]
                    - centered_ref[index, chunk, :] * sums_ref[1, chunk, :]
                )
                for tap, moved in windows(pad_ref.at[index], base, size, kernel):
                    term = jnp.sum((moved * d_conv).reshape(-1, SUBLANES, LANES), axis=0)
                    if base == 0:
                        part_ref[index, tap] = term
                    else:
                        part_ref[index, tap] += term
            place = pl.ds(pl.multiple_of(((step - steps) * blocks + index) * LANES, LANES), LANES)
            small_ref[:kernel, place] = jnp.sum(part_ref[index], axis=1)


def backward(cotangent, second, slope, centered, rstd, gain_mid, glu, kernel):
    rows, model = cotangent.shape
    steps = BACKWARD_STEPS
    width = model // steps
    blocks = width // LANES
    whole = lambda step: (0, 0)
    early = lambda step: (0, jnp.minimum(step, steps - 1))
    late = lambda step: (0, jnp.maximum(step - steps, 0))
    return pl.pallas_call(
        backward_kernel,
        grid=(2 * steps,),
        in_specs=[
            pl.BlockSpec((rows, model), whole),
            pl.BlockSpec((model, width), early),
            pl.BlockSpec((blocks, rows, LANES), lambda step: (jnp.minimum(step, steps - 1), 0, 0)),
            pl.BlockSpec((blocks, rows, LANES), lambda step: (lax.rem(step, steps), 0, 0)),
            pl.BlockSpec((rows, LANES), whole),
            pl.BlockSpec((1, width), early),
            pl.BlockSpec((rows, width), late),
        ],
        out_specs=pl.BlockSpec((kernel + 1, model), whole),
        out_shape=jax.ShapeDtypeStruct((kernel + 1, model), jnp.float32),
        scratch_shapes=[
            pltpu.VMEM((model // LANES, rows, LANES), jnp.float32),
            pltpu.VMEM((2, rows, LANES), jnp.float32),
            pltpu.VMEM((blocks, rows + 2 * EDGE, LANES), jnp.float32),
            pltpu.VMEM((blocks, kernel, SUBLANES, LANES), jnp.float32),
        ],
        compiler_params=pltpu.CompilerParams(vmem_limit_bytes=54 * 2**20),
        cost_estimate=pl.CostEstimate(
            flops=2 * rows * model * model + 20 * kernel * rows * model,
            bytes_accessed=2 * model * model + 12 * rows * model,
            transcendentals=rows * model,
        ),
        name="backward",
    )(cotangent, second, slope, centered, rstd, gain_mid.reshape(1, model), glu)


def spread(values, axis):
    copies = jnp.broadcast_to(values[None], (lax.axis_size(axis),) + values.shape)
    return lax.all_to_all(copies, axis, 0, 0, tiled=True)


def at(array, index, axis=0):
    return lax.dynamic_index_in_dim(array, index, axis, False)


def barrier(values):
    return lax.optimization_barrier(values)


def scatter_plane(values, owner, beside):
    owners = values.shape[0]
    side = 4 if owners % 4 == 0 else 1
    across, along = lax.rem(owner, side), lax.div(owner, side)
    values = values.reshape((owners // side, side) + values.shape[1:])
    total = at(values, across, 1)
    for k in range(1, side):
        moves = [(i, i // side * side + (i % side + k) % side) for i in range(owners)]
        total = total + lax.ppermute(at(values, lax.rem(across + k, side), 1), "dp", moves)
    count = owners // side
    values, beside = barrier((total, beside))
    total = at(values, along)
    for k in range(1, count):
        moves = [(i, (i // side + k) % count * side + i % side) for i in range(owners)]
        total = total + lax.ppermute(at(values, lax.rem(along + k, count)), "dp", moves)
    return total, beside


def body(fbank, lengths, sources, w_sub, gain_in, w_first, taps, gain_mid, w_second, cotangent):
    owners = lax.axis_size("dp")
    groups = lax.axis_size("fsdp")
    chips = groups // 2
    owner = lax.axis_index("dp")
    group = lax.axis_index("fsdp")
    core = lax.rem(group, 2)
    load, width = fbank.shape[2:]
    rows, model = cotangent.shape[2:]
    kernel = taps.shape[0]
    utt = lengths.shape[2]
    own_rows = w_second.shape[0]
    own = own_rows // owners

    swap = lambda block: lax.ppermute(block, "fsdp", [(i, i ^ 1) for i in range(groups)])

    first_t = lax.all_gather(w_first.T, "fsdp", axis=0, tiled=True)
    second = lax.all_gather(w_second, "fsdp", axis=0, tiled=True)

    meta = jnp.concatenate(
        [at(lengths, group).reshape(-1), at(sources, group).reshape(-1), jnp.stack([owner, group])]
    )
    blocks = send_rows(meta, fbank.reshape(load, width), utt, owners)
    received = lax.all_to_all(blocks, "dp", 0, 0, tiled=True)

    grad_out = cotangent.reshape(rows, model)
    grad_t = grad_out.T.reshape(chips, 2, owners, own, rows)
    of_core = lambda side: jnp.swapaxes(at(grad_t, side, 1), 0, 1).reshape(chips * own_rows, rows)
    left = jnp.concatenate([of_core(core), swap(of_core(1 - core))], axis=1)

    norm_in, x0, grad_spaced = front(meta, received, w_sub, gain_in, grad_out, utt, owners)
    norm_in, left = barrier((norm_in, left))
    glu, conv, mean, rstd, swished = forward(meta, norm_in, first_t, taps, gain_mid, rows, utt, owners)

    partial = dot(left, jnp.concatenate([swished, swap(swished)], axis=0)).astype(jnp.bfloat16)
    conv, partial = barrier((conv, partial))
    partial = lax.all_to_all(partial.reshape(owners, chips * own, model), "dp", 0, 0, tiled=True)

    gains = gain_mid.reshape(-1, 1, LANES)
    centered = (conv - mean) * rstd
    normed = centered * gains
    sig = sigmoid(normed)
    slope = gains * (sig * (1.0 + normed * (1.0 - sig)))
    small = backward(grad_spaced, second, slope, centered, rstd, gain_mid, glu, kernel)
    block = (x0.astype(jnp.float32) + dot_t(swished, second)).astype(jnp.bfloat16)

    small = small + swap(small)
    small, partial = scatter_plane(small.reshape(owners, -1, model), owner, partial)
    partial = jnp.sum(partial.astype(jnp.float32), axis=0).astype(jnp.bfloat16).reshape(chips, own, model)

    small = small.astype(jnp.bfloat16)
    both = jnp.concatenate([partial, jnp.broadcast_to(small[None], (chips,) + small.shape)], axis=1)
    same_core = [[2 * chip + side for chip in range(chips)] for side in range(2)]
    both = lax.all_to_all(both, "fsdp", 0, 0, tiled=True, axis_index_groups=same_core)
    both = jnp.sum(both.astype(jnp.float32), axis=0).astype(jnp.bfloat16)
    both = spread(both, "dp").astype(jnp.float32)
    grad_second = both[:, :own].reshape(own_rows, model)
    small = both[:, own:].reshape(kernel + 1, model)
    return (block.reshape(1, 1, rows, model), grad_second, small[:kernel], small[kernel])


def solution(mesh):
    in_specs = (
        P("dp", "fsdp", None, None),
        P(),
        P(),
        P(),
        P(),
        P(None, "fsdp"),
        P(),
        P(),
        P("fsdp", None),
        P("dp", "fsdp", None, None),
    )
    out_specs = (P("dp", "fsdp", None, None), P("fsdp", None), P(), P())
    return jax.shard_map(body, mesh=mesh, in_specs=in_specs, out_specs=out_specs, check_vma=False)
```

```python
import jax
import jax.numpy as jnp
from jax import lax
from jax.experimental import pallas as pl
from jax.experimental.pallas import tpu as pltpu
from jax.sharding import PartitionSpec as P

EDGE = 16
LANES = 128
SUBLANES = 8
FORWARD_STEPS = 6
BACKWARD_STEPS = 2
MOST = 104
CONTRACT_LAST = (((1,), (1,)), ((), ()))


def row_chunk(total):
    for size in (104, 96, 80, 64, 48, 32, 16, 8):
        if total % size == 0:
            return size
    return total


def windows(pad_ref, base, size, kernel):
    reach = EDGE - kernel // 2
    for phase in range(SUBLANES):
        taps = [tap for tap in range(kernel) if (tap + reach) % SUBLANES == phase]
        if not taps:
            continue
        last = (taps[-1] + reach) // SUBLANES * SUBLANES
        held = pad_ref[base + phase : base + phase + last + size, :]
        for tap in taps:
            start = (tap + reach) // SUBLANES * SUBLANES
            yield tap, held[start : start + size]


def fill_padded(pad_ref, values):
    rows, width = values.shape
    zeros = jnp.zeros((EDGE, LANES), jnp.float32)
    for index in range(width // LANES):
        pad_ref[index, :EDGE] = zeros
        pad_ref[index, EDGE + rows :] = zeros
        pad_ref[index, EDGE : EDGE + rows] = values[:, index * LANES : (index + 1) * LANES]


def sigmoid(values):
    return 0.5 * jnp.tanh(0.5 * values) + 0.5


def dot(left, right):
    return jnp.dot(left, right, preferred_element_type=jnp.float32)


def dot_t(left, right):
    return lax.dot_general(left, right, CONTRACT_LAST, preferred_element_type=jnp.float32)


def iotas(shape):
    return lax.broadcasted_iota(jnp.int32, shape, 0), lax.broadcasted_iota(jnp.int32, shape, 1)


def vmem(count):
    return [pl.BlockSpec(memory_space=pltpu.VMEM)] * count


def own_halves(meta_ref, utt, owners):
    owner = meta_ref[2 * utt * owners]
    return [lax.shift_right_logical(meta_ref[owner * utt + k], 1) for k in range(utt)]


def spaced_row(frame, halves):
    end = jnp.int32(0)
    moved = frame
    for half in halves[:-1]:
        end = end + 2 * half
        moved = moved + jnp.where(frame >= end, EDGE, 0)
    return moved


def send_kernel(utt, owners, meta_ref, fbank_ref, blocks_ref):
    count = utt * owners
    owner = meta_ref[2 * count]
    dest = [jnp.int32(0)] * utt
    length = [jnp.int32(0)] * utt
    for index in range(count):
        place = meta_ref[count + index] - owner * utt
        half = lax.shift_right_logical(meta_ref[index], 1)
        for j in range(utt):
            hit = place == j
            dest[j] = jnp.where(hit, index // utt, dest[j])
            length[j] = jnp.where(hit, half, length[j])
    row, column = iotas((MOST, fbank_ref.shape[0]))
    begin = jnp.int32(0)
    for j in range(utt):
        chosen = (column == row + begin).astype(jnp.bfloat16)
        blocks_ref[dest[j]] = dot(chosen, fbank_ref[...]).astype(jnp.bfloat16)
        begin = begin + length[j]


def send_rows(meta, fbank, utt, owners):
    return pl.pallas_call(
        lambda *refs: send_kernel(utt, owners, *refs),
        in_specs=[pl.BlockSpec(memory_space=pltpu.SMEM)] + vmem(1),
        out_specs=vmem(1)[0],
        out_shape=jax.ShapeDtypeStruct((owners, MOST, fbank.shape[1]), jnp.bfloat16),
        compiler_params=pltpu.CompilerParams(vmem_limit_bytes=12 * 2**20),
        cost_estimate=pl.CostEstimate(flops=2 * 3 * MOST * 300 * 640, bytes_accessed=2 * 2**20, transcendentals=0),
        name="send_rows",
    )(meta, fbank)


def front_kernel(
    utt, owners, meta_ref, received_ref, sub_ref, gain_ref, cotangent_ref,
    norm_ref, dense_ref, spaced_ref, wide_ref,
):
    count = utt * owners
    owner = meta_ref[2 * count]
    spaced, model = norm_ref.shape
    rows = dense_ref.shape[0]
    gap = EDGE // 2
    halves = own_halves(meta_ref, utt, owners)
    row, column = iotas((spaced // 2, MOST))
    start = jnp.int32(0)
    pairs = jnp.zeros((spaced // 2, received_ref.shape[2]), jnp.float32)
    for k in range(utt):
        chosen = ((row == column + start) & (column < halves[k])).astype(jnp.bfloat16)
        loader = lax.div(meta_ref[count + owner * utt + k], jnp.int32(utt))
        pairs = pairs + dot(chosen, received_ref[loader])
        start = start + halves[k] + gap
    values = sub_ref.shape[0]
    even = dot(pairs[:, :values].astype(jnp.bfloat16), sub_ref[...]).astype(jnp.bfloat16)
    odd = dot(pairs[:, values:].astype(jnp.bfloat16), sub_ref[...]).astype(jnp.bfloat16)

    row, column = iotas((spaced, spaced // 2))
    wide_ref[...] = dot((row == 2 * column).astype(jnp.bfloat16), even) + dot(
        (row == 2 * column + 1).astype(jnp.bfloat16), odd
    )
    depth = 4 * SUBLANES if spaced % (4 * SUBLANES) == 0 else 2 * SUBLANES

    def normalise(index, carry):
        chunk = pl.ds(pl.multiple_of(index * depth, depth), depth)
        values = wide_ref[chunk, :]
        mean = jnp.sum(values, axis=1, keepdims=True) / model
        values = values - mean
        spread = jnp.sum(values * values, axis=1, keepdims=True) / model
        norm_ref[chunk, :] = (values * lax.rsqrt(spread + 1e-05) * gain_ref[...]).astype(jnp.bfloat16)
        return carry

    lax.fori_loop(0, spaced // depth, normalise, 0)

    frame, column = iotas((rows, spaced // 2))
    moved = spaced_row(frame, halves)
    dense_ref[...] = (
        dot((moved == 2 * column).astype(jnp.bfloat16), even)
        + dot((moved == 2 * column + 1).astype(jnp.bfloat16), odd)
    ).astype(jnp.bfloat16)
    row, frame = iotas((spaced, rows))
    back = (spaced_row(frame, halves) == row).astype(jnp.bfloat16)
    spaced_ref[...] = dot(back, cotangent_ref[...]).astype(jnp.bfloat16)


def front(meta, received, w_sub, gain_in, cotangent, utt, owners):
    rows, model = cotangent.shape
    spaced = rows + EDGE * (utt - 1)
    bf16 = lambda *shape: jax.ShapeDtypeStruct(shape, jnp.bfloat16)
    return pl.pallas_call(
        lambda *refs: front_kernel(utt, owners, *refs),
        in_specs=[pl.BlockSpec(memory_space=pltpu.SMEM)] + vmem(4),
        out_specs=vmem(3),
        out_shape=[
            bf16(spaced, model), bf16(rows, model), bf16(spaced, model),
        ],
        scratch_shapes=[pltpu.VMEM((spaced, model), jnp.float32)],
        compiler_params=pltpu.CompilerParams(vmem_limit_bytes=32 * 2**20),
        cost_estimate=pl.CostEstimate(flops=4 * 10**9, bytes_accessed=16 * 2**20, transcendentals=0),
        name="front",
    )(meta, received, w_sub, gain_in.reshape(1, model), cotangent)


def forward_kernel(
    utt, owners, meta_ref, norm_ref, value_ref, gate_ref, taps_ref, gain_ref,
    glu_ref, conv_out_ref, mean_ref, rstd_ref, swished_ref, pad_ref, conv_ref, half_ref,
):
    step = pl.program_id(0)
    steps = pl.num_programs(0)
    rows, width = glu_ref.shape
    count = conv_ref.shape[0]
    blocks = width // LANES
    kernel = taps_ref.shape[0]
    @pl.when(step == 0)
    def _():
        mean_ref[...] = jnp.zeros_like(mean_ref)

    value = dot_t(norm_ref[...], value_ref[...])
    gate = dot_t(norm_ref[...], gate_ref[...])
    glu = (value * sigmoid(gate)).astype(jnp.bfloat16)
    glu_ref[...] = glu
    fill_padded(pad_ref, glu.astype(jnp.float32))
    size = row_chunk(rows)
    for index in range(blocks):
        lanes = slice(index * LANES, (index + 1) * LANES)
        for base in range(0, rows, size):
            total = jnp.zeros((size, LANES), jnp.float32)
            for tap, moved in windows(pad_ref.at[index], base, size, kernel):
                total = total + moved * taps_ref[tap : tap + 1, lanes]
            conv_ref[step * blocks + index, base : base + size, :] = total
            conv_out_ref[index, base : base + size, :] = total
            mean_ref[base : base + size, :] += total

    @pl.when(step == steps - 1)
    def _():
        model = count * LANES
        depth = 4 * SUBLANES if rows % (4 * SUBLANES) == 0 else 2 * SUBLANES

        def normalise(index, carry):
            chunk = pl.ds(pl.multiple_of(index * depth, depth), depth)
            parts = [conv_ref[block, chunk, :] for block in range(count)]
            mean = jnp.sum(mean_ref[chunk, :], axis=1, keepdims=True) / model
            mean_ref[chunk, :] = jnp.broadcast_to(mean, (depth, LANES))
            parts = [part - mean for part in parts]
            spread = jnp.sum(sum(part * part for part in parts), axis=1, keepdims=True) / model
            rstd = lax.rsqrt(spread + 1e-05)
            rstd_ref[chunk, :] = jnp.broadcast_to(rstd, (depth, LANES))
            for block in range(count):
                normed = parts[block] * rstd * gain_ref[:, block * LANES : (block + 1) * LANES]
                half_ref[block // blocks, chunk, block % blocks * LANES : (block % blocks + 1) * LANES] = (
                    normed * sigmoid(normed)
                ).astype(jnp.bfloat16)
            return carry

        lax.fori_loop(0, rows // depth, normalise, 0, unroll=True)
        frame, column = iotas((swished_ref.shape[0], rows))
        chosen = (spaced_row(frame, own_halves(meta_ref, utt, owners)) == column).astype(jnp.bfloat16)
        for slot in range(count // blocks):
            swished_ref[:, slot * width : (slot + 1) * width] = dot(chosen, half_ref[slot]).astype(jnp.bfloat16)


def forward(meta, norm_in, first_t, taps, gain_mid, dense, utt, owners):
    rows, model = norm_in.shape
    kernel = taps.shape[0]
    steps = FORWARD_STEPS
    width = model // steps
    whole = lambda step: (0, 0)
    return pl.pallas_call(
        lambda *refs: forward_kernel(utt, owners, *refs),
        grid=(steps,),
        in_specs=[
            pl.BlockSpec(memory_space=pltpu.SMEM),
            pl.BlockSpec((rows, model), whole),
            pl.BlockSpec((width, model), lambda step: (step, 0)),
            pl.BlockSpec((width, model), lambda step: (step + steps, 0)),
            pl.BlockSpec((kernel, width), lambda step: (0, step)),
            pl.BlockSpec((1, model), whole),
        ],
        out_specs=[
            pl.BlockSpec((rows, width), lambda step: (0, step)),
            pl.BlockSpec((width // LANES, rows, LANES), lambda step: (step, 0, 0)),
            pl.BlockSpec((rows, LANES), whole),
            pl.BlockSpec((rows, LANES), whole),
            pl.BlockSpec((dense, model), whole),
        ],
        out_shape=[
            jax.ShapeDtypeStruct((rows, model), jnp.bfloat16),
            jax.ShapeDtypeStruct((model // LANES, rows, LANES), jnp.float32),
            jax.ShapeDtypeStruct((rows, LANES), jnp.float32),
            jax.ShapeDtypeStruct((rows, LANES), jnp.float32),
            jax.ShapeDtypeStruct((dense, model), jnp.bfloat16),
        ],
        scratch_shapes=[
            pltpu.VMEM((width // LANES, rows + 2 * EDGE, LANES), jnp.float32),
            pltpu.VMEM((model // LANES, rows, LANES), jnp.float32),
            pltpu.VMEM((steps, rows, width), jnp.bfloat16),
        ],
        compiler_params=pltpu.CompilerParams(vmem_limit_bytes=50 * 2**20),
        cost_estimate=pl.CostEstimate(
            flops=4 * rows * model * model + 20 * kernel * rows * model,
            bytes_accessed=4 * model * model + 10 * rows * model,
            transcendentals=2 * rows * model,
        ),
        name="forward",
    )(meta, norm_in, first_t, first_t, taps, gain_mid.reshape(1, model))


def backward_kernel(
    cotangent_ref, second_ref, slope_ref, centered_ref, rstd_ref, gain_ref, glu_ref,
    small_ref, scaled_ref, sums_ref, pad_ref, part_ref,
):
    step = pl.program_id(0)
    steps = pl.num_programs(0) // 2
    rows, width = glu_ref.shape
    kernel = small_ref.shape[0] - 1
    blocks = width // LANES
    model = steps * width

    @pl.when(step == 0)
    def _():
        sums_ref[...] = jnp.zeros_like(sums_ref)

    @pl.when(step < steps)
    def _():
        d_swished = dot(cotangent_ref[...], second_ref[...])
        for index in range(blocks):
            scaled_ref[step * blocks + index] = d_swished[:, index * LANES : (index + 1) * LANES]
        depth = 4 * SUBLANES if rows % (4 * SUBLANES) == 0 else 2 * SUBLANES

        def chunk_step(number, totals):
            chunk = pl.ds(pl.multiple_of(number * depth, depth), depth)
            first = sums_ref[0, chunk, :]
            second = sums_ref[1, chunk, :]
            result = []
            for index in range(blocks):
                place = step * blocks + index
                scaled = scaled_ref[place, chunk, :] * slope_ref[index, chunk, :]
                scaled_ref[place, chunk, :] = scaled
                both = scaled * centered_ref[index, chunk, :]
                first = first + scaled
                second = second + both
                result.append(totals[index] + jnp.sum(both.reshape(-1, SUBLANES, LANES), axis=0))
            sums_ref[0, chunk, :] = first
            sums_ref[1, chunk, :] = second
            return tuple(result)

        zero = jnp.zeros((SUBLANES, LANES), jnp.float32)
        totals = lax.fori_loop(0, rows // depth, chunk_step, (zero,) * blocks)
        for index in range(blocks):
            lanes = slice(index * LANES, (index + 1) * LANES)
            place = pl.ds(pl.multiple_of((step * blocks + index) * LANES, LANES), LANES)
            small_ref[kernel:, place] = jnp.sum(totals[index], axis=0, keepdims=True) / gain_ref[:, lanes]

    @pl.when(step == steps)
    def _():
        for index in range(2):
            mean = jnp.sum(sums_ref[index], axis=1, keepdims=True) / model
            sums_ref[index] = jnp.broadcast_to(mean, (rows, LANES))

    @pl.when(step >= steps)
    def _():
        fill_padded(pad_ref, glu_ref[...].astype(jnp.float32))
        size = row_chunk(rows)
        for index in range(blocks):
            for base in range(0, rows, size):
                chunk = slice(base, base + size)
                d_conv = rstd_ref[chunk, :] * (
                    scaled_ref[(step - steps) * blocks + index, chunk, :]
                    - sums_ref[0, chunk, :]
                    - centered_ref[index, chunk, :] * sums_ref[1, chunk, :]
                )
                for tap, moved in windows(pad_ref.at[index], base, size, kernel):
                    term = jnp.sum((moved * d_conv).reshape(-1, SUBLANES, LANES), axis=0)
                    if base == 0:
                        part_ref[index, tap] = term
                    else:
                        part_ref[index, tap] += term
            place = pl.ds(pl.multiple_of(((step - steps) * blocks + index) * LANES, LANES), LANES)
            small_ref[:kernel, place] = jnp.sum(part_ref[index], axis=1)


def backward(cotangent, second, slope, centered, rstd, gain_mid, glu, kernel):
    rows, model = cotangent.shape
    steps = BACKWARD_STEPS
    width = model // steps
    blocks = width // LANES
    whole = lambda step: (0, 0)
    early = lambda step: (0, jnp.minimum(step, steps - 1))
    late = lambda step: (0, jnp.maximum(step - steps, 0))
    return pl.pallas_call(
        backward_kernel,
        grid=(2 * steps,),
        in_specs=[
            pl.BlockSpec((rows, model), whole),
            pl.BlockSpec((model, width), early),
            pl.BlockSpec((blocks, rows, LANES), lambda step: (jnp.minimum(step, steps - 1), 0, 0)),
            pl.BlockSpec((blocks, rows, LANES), lambda step: (lax.rem(step, steps), 0, 0)),
            pl.BlockSpec((rows, LANES), whole),
            pl.BlockSpec((1, width), early),
            pl.BlockSpec((rows, width), late),
        ],
        out_specs=pl.BlockSpec((kernel + 1, model), whole),
        out_shape=jax.ShapeDtypeStruct((kernel + 1, model), jnp.float32),
        scratch_shapes=[
            pltpu.VMEM((model // LANES, rows, LANES), jnp.float32),
            pltpu.VMEM((2, rows, LANES), jnp.float32),
            pltpu.VMEM((blocks, rows + 2 * EDGE, LANES), jnp.float32),
            pltpu.VMEM((blocks, kernel, SUBLANES, LANES), jnp.float32),
        ],
        compiler_params=pltpu.CompilerParams(vmem_limit_bytes=54 * 2**20),
        cost_estimate=pl.CostEstimate(
            flops=2 * rows * model * model + 20 * kernel * rows * model,
            bytes_accessed=2 * model * model + 12 * rows * model,
            transcendentals=rows * model,
        ),
        name="backward",
    )(cotangent, second, slope, centered, rstd, gain_mid.reshape(1, model), glu)


def total_kernel(pieces_ref, out_ref):
    total = pieces_ref[0].astype(jnp.float32)
    for index in range(1, pieces_ref.shape[0]):
        total = total + pieces_ref[index].astype(jnp.float32)
    out_ref[...] = total.astype(jnp.bfloat16)


def total_of(pieces):
    count, rows, model = pieces.shape
    width = model // 3
    return pl.pallas_call(
        total_kernel,
        grid=(3,),
        in_specs=[pl.BlockSpec((count, rows, width), lambda step: (0, 0, step))],
        out_specs=pl.BlockSpec((rows, width), lambda step: (0, step)),
        out_shape=jax.ShapeDtypeStruct((rows, model), jnp.bfloat16),
        compiler_params=pltpu.CompilerParams(vmem_limit_bytes=12 * 2**20),
        cost_estimate=pl.CostEstimate(flops=count * rows * model, bytes_accessed=2 * count * rows * model, transcendentals=0),
        name="total",
    )(pieces)


def outputs_kernel(own, both_ref, large_ref, taps_ref, gain_ref):
    owners, both_rows, model = both_ref.shape
    kernel = taps_ref.shape[0]
    share = both_rows - own
    for owner in range(owners):
        block = both_ref[owner].astype(jnp.float32)
        large_ref[owner * own : (owner + 1) * own, :] = block[:own]
        for index in range(share):
            row = owner * share + index
            if row < kernel:
                taps_ref[row : row + 1, :] = block[own + index : own + index + 1]
            else:
                gain_ref[...] = block[own + index : own + index + 1]


def outputs(both, own, kernel):
    owners, _, model = both.shape
    f32 = lambda *shape: jax.ShapeDtypeStruct(shape, jnp.float32)
    return pl.pallas_call(
        lambda *refs: outputs_kernel(own, *refs),
        in_specs=vmem(1),
        out_specs=vmem(3),
        out_shape=[f32(owners * own, model), f32(kernel, model), f32(1, model)],
        compiler_params=pltpu.CompilerParams(vmem_limit_bytes=12 * 2**20),
        name="outputs",
    )(both)


def spread(values, axis):
    copies = jnp.broadcast_to(values[None], (lax.axis_size(axis),) + values.shape)
    return lax.all_to_all(copies, axis, 0, 0, tiled=True)


def at(array, index, axis=0):
    return lax.dynamic_index_in_dim(array, index, axis, False)


def barrier(values):
    return lax.optimization_barrier(values)


def scatter_plane(values, owner, beside):
    owners = values.shape[0]
    side = 4 if owners % 4 == 0 else 1
    across, along = lax.rem(owner, side), lax.div(owner, side)
    values = values.reshape((owners // side, side) + values.shape[1:])
    total = at(values, across, 1)
    for k in range(1, side):
        moves = [(i, i // side * side + (i % side + k) % side) for i in range(owners)]
        total = total + lax.ppermute(at(values, lax.rem(across + k, side), 1), "dp", moves)
    count = owners // side
    values, beside = barrier((total, beside))
    total = at(values, along)
    for k in range(1, count):
        moves = [(i, (i // side + k) % count * side + i % side) for i in range(owners)]
        total = total + lax.ppermute(at(values, lax.rem(along + k, count)), "dp", moves)
    return total, beside


def body(fbank, lengths, sources, w_sub, gain_in, w_first, taps, gain_mid, w_second, cotangent):
    owners = lax.axis_size("dp")
    groups = lax.axis_size("fsdp")
    chips = groups // 2
    owner = lax.axis_index("dp")
    group = lax.axis_index("fsdp")
    core = lax.rem(group, 2)
    load, width = fbank.shape[2:]
    rows, model = cotangent.shape[2:]
    kernel = taps.shape[0]
    utt = lengths.shape[2]
    own_rows = w_second.shape[0]
    own = own_rows // owners

    swap = lambda block: lax.ppermute(block, "fsdp", [(i, i ^ 1) for i in range(groups)])

    first_t = lax.all_gather(w_first.T, "fsdp", axis=0, tiled=True)
    second = lax.all_gather(w_second, "fsdp", axis=0, tiled=True)

    meta = jnp.concatenate(
        [at(lengths, group).reshape(-1), at(sources, group).reshape(-1), jnp.stack([owner, group])]
    )
    blocks = send_rows(meta, fbank.reshape(load, width), utt, owners)
    received = lax.all_to_all(blocks, "dp", 0, 0, tiled=True)

    grad_out = cotangent.reshape(rows, model)
    grad_t = grad_out.T.reshape(chips, 2, owners, own, rows)
    of_core = lambda side: jnp.swapaxes(at(grad_t, side, 1), 0, 1).reshape(chips * own_rows, rows)
    left = jnp.concatenate([of_core(core), swap(of_core(1 - core))], axis=1)

    norm_in, x0, grad_spaced = front(meta, received, w_sub, gain_in, grad_out, utt, owners)
    norm_in, left = barrier((norm_in, left))
    glu, conv, mean, rstd, swished = forward(meta, norm_in, first_t, taps, gain_mid, rows, utt, owners)

    partial = dot(left, jnp.concatenate([swished, swap(swished)], axis=0)).astype(jnp.bfloat16)
    conv, partial = barrier((conv, partial))
    partial = lax.all_to_all(partial.reshape(owners, chips * own, model), "dp", 0, 0, tiled=True)

    gains = gain_mid.reshape(-1, 1, LANES)
    centered = (conv - mean) * rstd
    normed = centered * gains
    sig = sigmoid(normed)
    slope = gains * (sig * (1.0 + normed * (1.0 - sig)))
    small = backward(grad_spaced, second, slope, centered, rstd, gain_mid, glu, kernel)
    block = (x0.astype(jnp.float32) + dot_t(swished, second)).astype(jnp.bfloat16)

    small = small + swap(small)
    small, partial = scatter_plane(small.reshape(owners, -1, model), owner, partial)
    partial = total_of(partial).reshape(chips, own, model)

    small = small.astype(jnp.bfloat16)
    both = jnp.concatenate([partial, jnp.broadcast_to(small[None], (chips,) + small.shape)], axis=1)
    same_core = [[2 * chip + side for chip in range(chips)] for side in range(2)]
    both = lax.all_to_all(both, "fsdp", 0, 0, tiled=True, axis_index_groups=same_core)
    both = jnp.sum(both.astype(jnp.float32), axis=0).astype(jnp.bfloat16)
    grad_second, grad_taps, grad_gain = outputs(spread(both, "dp"), own, kernel)
    return (block.reshape(1, 1, rows, model), grad_second, grad_taps, grad_gain.reshape(model))


def solution(mesh):
    in_specs = (
        P("dp", "fsdp", None, None),
        P(),
        P(),
        P(),
        P(),
        P(None, "fsdp"),
        P(),
        P(),
        P("fsdp", None),
        P("dp", "fsdp", None, None),
    )
    out_specs = (P("dp", "fsdp", None, None), P("fsdp", None), P(), P())
    return jax.shard_map(body, mesh=mesh, in_specs=in_specs, out_specs=out_specs, check_vma=False)
```

```python
import jax
import jax.numpy as jnp
from jax import lax
from jax.experimental import pallas as pl
from jax.experimental.pallas import tpu as pltpu
from jax.sharding import PartitionSpec as P

EDGE = 16
LANES = 128
SUBLANES = 8
FORWARD_STEPS = 6
BACKWARD_STEPS = 2
MOST = 104
CONTRACT_LAST = (((1,), (1,)), ((), ()))


def row_chunk(total):
    for size in (104, 96, 80, 64, 48, 32, 16, 8):
        if total % size == 0:
            return size
    return total


def windows(pad_ref, base, size, kernel):
    reach = EDGE - kernel // 2
    for phase in range(SUBLANES):
        taps = [tap for tap in range(kernel) if (tap + reach) % SUBLANES == phase]
        if not taps:
            continue
        last = (taps[-1] + reach) // SUBLANES * SUBLANES
        held = pad_ref[base + phase : base + phase + last + size, :]
        for tap in taps:
            start = (tap + reach) // SUBLANES * SUBLANES
            yield tap, held[start : start + size]


def fill_padded(pad_ref, values):
    rows, width = values.shape
    zeros = jnp.zeros((EDGE, LANES), jnp.float32)
    for index in range(width // LANES):
        pad_ref[index, :EDGE] = zeros
        pad_ref[index, EDGE + rows :] = zeros
        pad_ref[index, EDGE : EDGE + rows] = values[:, index * LANES : (index + 1) * LANES]


def sigmoid(values):
    return 0.5 * jnp.tanh(0.5 * values) + 0.5


def dot(left, right):
    return jnp.dot(left, right, preferred_element_type=jnp.float32)


def dot_t(left, right):
    return lax.dot_general(left, right, CONTRACT_LAST, preferred_element_type=jnp.float32)


def iotas(shape):
    return lax.broadcasted_iota(jnp.int32, shape, 0), lax.broadcasted_iota(jnp.int32, shape, 1)


def vmem(count):
    return [pl.BlockSpec(memory_space=pltpu.VMEM)] * count


def own_halves(meta_ref, utt, owners):
    owner = meta_ref[2 * utt * owners]
    return [lax.shift_right_logical(meta_ref[owner * utt + k], 1) for k in range(utt)]


def spaced_row(frame, halves):
    end = jnp.int32(0)
    moved = frame
    for half in halves[:-1]:
        end = end + 2 * half
        moved = moved + jnp.where(frame >= end, EDGE, 0)
    return moved


def send_kernel(utt, owners, meta_ref, fbank_ref, blocks_ref):
    count = utt * owners
    owner = meta_ref[2 * count]
    dest = [jnp.int32(0)] * utt
    length = [jnp.int32(0)] * utt
    for index in range(count):
        place = meta_ref[count + index] - owner * utt
        half = lax.shift_right_logical(meta_ref[index], 1)
        for j in range(utt):
            hit = place == j
            dest[j] = jnp.where(hit, index // utt, dest[j])
            length[j] = jnp.where(hit, half, length[j])
    row, column = iotas((MOST, fbank_ref.shape[0]))
    begin = jnp.int32(0)
    for j in range(utt):
        chosen = (column == row + begin).astype(jnp.bfloat16)
        blocks_ref[dest[j]] = dot(chosen, fbank_ref[...]).astype(jnp.bfloat16)
        begin = begin + length[j]


def send_rows(meta, fbank, utt, owners):
    return pl.pallas_call(
        lambda *refs: send_kernel(utt, owners, *refs),
        in_specs=[pl.BlockSpec(memory_space=pltpu.SMEM)] + vmem(1),
        out_specs=vmem(1)[0],
        out_shape=jax.ShapeDtypeStruct((owners, MOST, fbank.shape[1]), jnp.bfloat16),
        compiler_params=pltpu.CompilerParams(vmem_limit_bytes=12 * 2**20),
        cost_estimate=pl.CostEstimate(flops=2 * 3 * MOST * 300 * 640, bytes_accessed=2 * 2**20, transcendentals=0),
        name="send_rows",
    )(meta, fbank)


def front_kernel(
    utt, owners, meta_ref, received_ref, sub_ref, gain_ref, cotangent_ref,
    norm_ref, dense_ref, spaced_ref, wide_ref,
):
    count = utt * owners
    owner = meta_ref[2 * count]
    spaced, model = norm_ref.shape
    rows = dense_ref.shape[0]
    gap = EDGE // 2
    halves = own_halves(meta_ref, utt, owners)
    row, column = iotas((spaced // 2, MOST))
    start = jnp.int32(0)
    pairs = jnp.zeros((spaced // 2, received_ref.shape[2]), jnp.float32)
    for k in range(utt):
        chosen = ((row == column + start) & (column < halves[k])).astype(jnp.bfloat16)
        loader = lax.div(meta_ref[count + owner * utt + k], jnp.int32(utt))
        pairs = pairs + dot(chosen, received_ref[loader])
        start = start + halves[k] + gap
    values = sub_ref.shape[0]
    even = dot(pairs[:, :values].astype(jnp.bfloat16), sub_ref[...]).astype(jnp.bfloat16)
    odd = dot(pairs[:, values:].astype(jnp.bfloat16), sub_ref[...]).astype(jnp.bfloat16)

    row, column = iotas((spaced, spaced // 2))
    wide_ref[...] = dot((row == 2 * column).astype(jnp.bfloat16), even) + dot(
        (row == 2 * column + 1).astype(jnp.bfloat16), odd
    )
    depth = 4 * SUBLANES if spaced % (4 * SUBLANES) == 0 else 2 * SUBLANES

    def normalise(index, carry):
        chunk = pl.ds(pl.multiple_of(index * depth, depth), depth)
        values = wide_ref[chunk, :]
        mean = jnp.sum(values, axis=1, keepdims=True) / model
        values = values - mean
        spread = jnp.sum(values * values, axis=1, keepdims=True) / model
        norm_ref[chunk, :] = (values * lax.rsqrt(spread + 1e-05) * gain_ref[...]).astype(jnp.bfloat16)
        return carry

    lax.fori_loop(0, spaced // depth, normalise, 0)

    frame, column = iotas((rows, spaced // 2))
    moved = spaced_row(frame, halves)
    dense_ref[...] = (
        dot((moved == 2 * column).astype(jnp.bfloat16), even)
        + dot((moved == 2 * column + 1).astype(jnp.bfloat16), odd)
    ).astype(jnp.bfloat16)
    row, frame = iotas((spaced, rows))
    back = (spaced_row(frame, halves) == row).astype(jnp.bfloat16)
    spaced_ref[...] = dot(back, cotangent_ref[...]).astype(jnp.bfloat16)


def front(meta, received, w_sub, gain_in, cotangent, utt, owners):
    rows, model = cotangent.shape
    spaced = rows + EDGE * (utt - 1)
    bf16 = lambda *shape: jax.ShapeDtypeStruct(shape, jnp.bfloat16)
    return pl.pallas_call(
        lambda *refs: front_kernel(utt, owners, *refs),
        in_specs=[pl.BlockSpec(memory_space=pltpu.SMEM)] + vmem(4),
        out_specs=vmem(3),
        out_shape=[
            bf16(spaced, model), bf16(rows, model), bf16(spaced, model),
        ],
        scratch_shapes=[pltpu.VMEM((spaced, model), jnp.float32)],
        compiler_params=pltpu.CompilerParams(vmem_limit_bytes=32 * 2**20),
        cost_estimate=pl.CostEstimate(flops=4 * 10**9, bytes_accessed=16 * 2**20, transcendentals=0),
        name="front",
    )(meta, received, w_sub, gain_in.reshape(1, model), cotangent)


def forward_kernel(
    utt, owners, meta_ref, norm_ref, value_ref, gate_ref, taps_ref, gain_ref,
    glu_ref, conv_out_ref, mean_ref, rstd_ref, swished_ref, pad_ref, conv_ref, half_ref,
):
    step = pl.program_id(0)
    steps = pl.num_programs(0)
    rows, width = glu_ref.shape
    count = conv_ref.shape[0]
    blocks = width // LANES
    kernel = taps_ref.shape[0]
    @pl.when(step == 0)
    def _():
        mean_ref[...] = jnp.zeros_like(mean_ref)

    value = dot_t(norm_ref[...], value_ref[...])
    gate = dot_t(norm_ref[...], gate_ref[...])
    glu = (value * sigmoid(gate)).astype(jnp.bfloat16)
    glu_ref[...] = glu
    fill_padded(pad_ref, glu.astype(jnp.float32))
    size = row_chunk(rows)
    for index in range(blocks):
        lanes = slice(index * LANES, (index + 1) * LANES)
        for base in range(0, rows, size):
            total = jnp.zeros((size, LANES), jnp.float32)
            for tap, moved in windows(pad_ref.at[index], base, size, kernel):
                total = total + moved * taps_ref[tap : tap + 1, lanes]
            conv_ref[step * blocks + index, base : base + size, :] = total
            conv_out_ref[index, base : base + size, :] = total
            mean_ref[base : base + size, :] += total

    @pl.when(step == steps - 1)
    def _():
        model = count * LANES
        depth = 4 * SUBLANES if rows % (4 * SUBLANES) == 0 else 2 * SUBLANES

        def normalise(index, carry):
            chunk = pl.ds(pl.multiple_of(index * depth, depth), depth)
            parts = [conv_ref[block, chunk, :] for block in range(count)]
            mean = jnp.sum(mean_ref[chunk, :], axis=1, keepdims=True) / model
            mean_ref[chunk, :] = jnp.broadcast_to(mean, (depth, LANES))
            parts = [part - mean for part in parts]
            spread = jnp.sum(sum(part * part for part in parts), axis=1, keepdims=True) / model
            rstd = lax.rsqrt(spread + 1e-05)
            rstd_ref[chunk, :] = jnp.broadcast_to(rstd, (depth, LANES))
            for block in range(count):
                normed = parts[block] * rstd * gain_ref[:, block * LANES : (block + 1) * LANES]
                half_ref[block // blocks, chunk, block % blocks * LANES : (block % blocks + 1) * LANES] = (
                    normed * sigmoid(normed)
                ).astype(jnp.bfloat16)
            return carry

        lax.fori_loop(0, rows // depth, normalise, 0, unroll=True)
        frame, column = iotas((swished_ref.shape[0], rows))
        chosen = (spaced_row(frame, own_halves(meta_ref, utt, owners)) == column).astype(jnp.bfloat16)
        for slot in range(count // blocks):
            swished_ref[:, slot * width : (slot + 1) * width] = dot(chosen, half_ref[slot]).astype(jnp.bfloat16)


def forward(meta, norm_in, first_t, taps, gain_mid, dense, utt, owners):
    rows, model = norm_in.shape
    kernel = taps.shape[0]
    steps = FORWARD_STEPS
    width = model // steps
    whole = lambda step: (0, 0)
    return pl.pallas_call(
        lambda *refs: forward_kernel(utt, owners, *refs),
        grid=(steps,),
        in_specs=[
            pl.BlockSpec(memory_space=pltpu.SMEM),
            pl.BlockSpec((rows, model), whole),
            pl.BlockSpec((width, model), lambda step: (step, 0)),
            pl.BlockSpec((width, model), lambda step: (step + steps, 0)),
            pl.BlockSpec((kernel, width), lambda step: (0, step)),
            pl.BlockSpec((1, model), whole),
        ],
        out_specs=[
            pl.BlockSpec((rows, width), lambda step: (0, step)),
            pl.BlockSpec((width // LANES, rows, LANES), lambda step: (step, 0, 0)),
            pl.BlockSpec((rows, LANES), whole),
            pl.BlockSpec((rows, LANES), whole),
            pl.BlockSpec((dense, model), whole),
        ],
        out_shape=[
            jax.ShapeDtypeStruct((rows, model), jnp.bfloat16),
            jax.ShapeDtypeStruct((model // LANES, rows, LANES), jnp.float32),
            jax.ShapeDtypeStruct((rows, LANES), jnp.float32),
            jax.ShapeDtypeStruct((rows, LANES), jnp.float32),
            jax.ShapeDtypeStruct((dense, model), jnp.bfloat16),
        ],
        scratch_shapes=[
            pltpu.VMEM((width // LANES, rows + 2 * EDGE, LANES), jnp.float32),
            pltpu.VMEM((model // LANES, rows, LANES), jnp.float32),
            pltpu.VMEM((steps, rows, width), jnp.bfloat16),
        ],
        compiler_params=pltpu.CompilerParams(vmem_limit_bytes=50 * 2**20),
        cost_estimate=pl.CostEstimate(
            flops=4 * rows * model * model + 20 * kernel * rows * model,
            bytes_accessed=4 * model * model + 10 * rows * model,
            transcendentals=2 * rows * model,
        ),
        name="forward",
    )(meta, norm_in, first_t, first_t, taps, gain_mid.reshape(1, model))


def backward_kernel(
    cotangent_ref, second_ref, slope_ref, centered_ref, rstd_ref, gain_ref, glu_ref,
    small_ref, scaled_ref, sums_ref, pad_ref, part_ref,
):
    step = pl.program_id(0)
    steps = pl.num_programs(0) // 2
    rows, width = glu_ref.shape
    kernel = small_ref.shape[0] - 1
    blocks = width // LANES
    model = steps * width

    @pl.when(step == 0)
    def _():
        sums_ref[...] = jnp.zeros_like(sums_ref)

    @pl.when(step < steps)
    def _():
        d_swished = dot(cotangent_ref[...], second_ref[...])
        for index in range(blocks):
            scaled_ref[step * blocks + index] = d_swished[:, index * LANES : (index + 1) * LANES]
        depth = 4 * SUBLANES if rows % (4 * SUBLANES) == 0 else 2 * SUBLANES

        def chunk_step(number, totals):
            chunk = pl.ds(pl.multiple_of(number * depth, depth), depth)
            first = sums_ref[0, chunk, :]
            second = sums_ref[1, chunk, :]
            result = []
            for index in range(blocks):
                place = step * blocks + index
                scaled = scaled_ref[place, chunk, :] * slope_ref[index, chunk, :]
                scaled_ref[place, chunk, :] = scaled
                both = scaled * centered_ref[index, chunk, :]
                first = first + scaled
                second = second + both
                result.append(totals[index] + jnp.sum(both.reshape(-1, SUBLANES, LANES), axis=0))
            sums_ref[0, chunk, :] = first
            sums_ref[1, chunk, :] = second
            return tuple(result)

        zero = jnp.zeros((SUBLANES, LANES), jnp.float32)
        totals = lax.fori_loop(0, rows // depth, chunk_step, (zero,) * blocks)
        for index in range(blocks):
            lanes = slice(index * LANES, (index + 1) * LANES)
            place = pl.ds(pl.multiple_of((step * blocks + index) * LANES, LANES), LANES)
            small_ref[kernel:, place] = jnp.sum(totals[index], axis=0, keepdims=True) / gain_ref[:, lanes]

    @pl.when(step == steps)
    def _():
        for index in range(2):
            mean = jnp.sum(sums_ref[index], axis=1, keepdims=True) / model
            sums_ref[index] = jnp.broadcast_to(mean, (rows, LANES))

    @pl.when(step >= steps)
    def _():
        fill_padded(pad_ref, glu_ref[...].astype(jnp.float32))
        size = row_chunk(rows)
        for index in range(blocks):
            for base in range(0, rows, size):
                chunk = slice(base, base + size)
                d_conv = rstd_ref[chunk, :] * (
                    scaled_ref[(step - steps) * blocks + index, chunk, :]
                    - sums_ref[0, chunk, :]
                    - centered_ref[index, chunk, :] * sums_ref[1, chunk, :]
                )
                for tap, moved in windows(pad_ref.at[index], base, size, kernel):
                    term = jnp.sum((moved * d_conv).reshape(-1, SUBLANES, LANES), axis=0)
                    if base == 0:
                        part_ref[index, tap] = term
                    else:
                        part_ref[index, tap] += term
            place = pl.ds(pl.multiple_of(((step - steps) * blocks + index) * LANES, LANES), LANES)
            small_ref[:kernel, place] = jnp.sum(part_ref[index], axis=1)


def backward(cotangent, second, slope, centered, rstd, gain_mid, glu, kernel):
    rows, model = cotangent.shape
    steps = BACKWARD_STEPS
    width = model // steps
    blocks = width // LANES
    whole = lambda step: (0, 0)
    early = lambda step: (0, jnp.minimum(step, steps - 1))
    late = lambda step: (0, jnp.maximum(step - steps, 0))
    return pl.pallas_call(
        backward_kernel,
        grid=(2 * steps,),
        in_specs=[
            pl.BlockSpec((rows, model), whole),
            pl.BlockSpec((model, width), early),
            pl.BlockSpec((blocks, rows, LANES), lambda step: (jnp.minimum(step, steps - 1), 0, 0)),
            pl.BlockSpec((blocks, rows, LANES), lambda step: (lax.rem(step, steps), 0, 0)),
            pl.BlockSpec((rows, LANES), whole),
            pl.BlockSpec((1, width), early),
            pl.BlockSpec((rows, width), late),
        ],
        out_specs=pl.BlockSpec((kernel + 1, model), whole),
        out_shape=jax.ShapeDtypeStruct((kernel + 1, model), jnp.float32),
        scratch_shapes=[
            pltpu.VMEM((model // LANES, rows, LANES), jnp.float32),
            pltpu.VMEM((2, rows, LANES), jnp.float32),
            pltpu.VMEM((blocks, rows + 2 * EDGE, LANES), jnp.float32),
            pltpu.VMEM((blocks, kernel, SUBLANES, LANES), jnp.float32),
        ],
        compiler_params=pltpu.CompilerParams(vmem_limit_bytes=54 * 2**20),
        cost_estimate=pl.CostEstimate(
            flops=2 * rows * model * model + 20 * kernel * rows * model,
            bytes_accessed=2 * model * model + 12 * rows * model,
            transcendentals=rows * model,
        ),
        name="backward",
    )(cotangent, second, slope, centered, rstd, gain_mid.reshape(1, model), glu)


def total_kernel(pieces_ref, out_ref):
    total = pieces_ref[0].astype(jnp.float32)
    for index in range(1, pieces_ref.shape[0]):
        total = total + pieces_ref[index].astype(jnp.float32)
    out_ref[...] = total.astype(jnp.bfloat16)


def total_of(pieces):
    count, rows, model = pieces.shape
    width = model // 3
    return pl.pallas_call(
        total_kernel,
        grid=(3,),
        in_specs=[pl.BlockSpec((count, rows, width), lambda step: (0, 0, step))],
        out_specs=pl.BlockSpec((rows, width), lambda step: (0, step)),
        out_shape=jax.ShapeDtypeStruct((rows, model), jnp.bfloat16),
        compiler_params=pltpu.CompilerParams(vmem_limit_bytes=12 * 2**20),
        cost_estimate=pl.CostEstimate(flops=count * rows * model, bytes_accessed=2 * count * rows * model, transcendentals=0),
        name="total",
    )(pieces)


def outputs_kernel(own, both_ref, large_ref, taps_ref, gain_ref):
    owners, both_rows, model = both_ref.shape
    kernel = taps_ref.shape[0]
    share = both_rows - own
    for owner in range(owners):
        block = both_ref[owner].astype(jnp.float32)
        large_ref[owner * own : (owner + 1) * own, :] = block[:own]
        for index in range(share):
            row = owner * share + index
            if row < kernel:
                taps_ref[row : row + 1, :] = block[own + index : own + index + 1]
            else:
                gain_ref[...] = block[own + index]


def outputs(both, own, kernel):
    owners, _, model = both.shape
    f32 = lambda *shape: jax.ShapeDtypeStruct(shape, jnp.float32)
    return pl.pallas_call(
        lambda *refs: outputs_kernel(own, *refs),
        in_specs=vmem(1),
        out_specs=vmem(3),
        out_shape=[f32(owners * own, model), f32(kernel, model), f32(model)],
        compiler_params=pltpu.CompilerParams(vmem_limit_bytes=12 * 2**20),
        name="outputs",
    )(both)


def spread(values, axis):
    copies = jnp.broadcast_to(values[None], (lax.axis_size(axis),) + values.shape)
    return lax.all_to_all(copies, axis, 0, 0, tiled=True)


def at(array, index, axis=0):
    return lax.dynamic_index_in_dim(array, index, axis, False)


def barrier(values):
    return lax.optimization_barrier(values)


def scatter_plane(values, owner, beside):
    owners = values.shape[0]
    side = 4 if owners % 4 == 0 else 1
    across, along = lax.rem(owner, side), lax.div(owner, side)
    values = values.reshape((owners // side, side) + values.shape[1:])
    total = at(values, across, 1)
    for k in range(1, side):
        moves = [(i, i // side * side + (i % side + k) % side) for i in range(owners)]
        total = total + lax.ppermute(at(values, lax.rem(across + k, side), 1), "dp", moves)
    count = owners // side
    values, beside = barrier((total, beside))
    total = at(values, along)
    for k in range(1, count):
        moves = [(i, (i // side + k) % count * side + i % side) for i in range(owners)]
        total = total + lax.ppermute(at(values, lax.rem(along + k, count)), "dp", moves)
    return total, beside


def body(fbank, lengths, sources, w_sub, gain_in, w_first, taps, gain_mid, w_second, cotangent):
    owners = lax.axis_size("dp")
    groups = lax.axis_size("fsdp")
    chips = groups // 2
    owner = lax.axis_index("dp")
    group = lax.axis_index("fsdp")
    core = lax.rem(group, 2)
    load, width = fbank.shape[2:]
    rows, model = cotangent.shape[2:]
    kernel = taps.shape[0]
    utt = lengths.shape[2]
    own_rows = w_second.shape[0]
    own = own_rows // owners

    swap = lambda block: lax.ppermute(block, "fsdp", [(i, i ^ 1) for i in range(groups)])

    first_t = lax.all_gather(w_first.T, "fsdp", axis=0, tiled=True)
    second = lax.all_gather(w_second, "fsdp", axis=0, tiled=True)

    meta = jnp.concatenate(
        [at(lengths, group).reshape(-1), at(sources, group).reshape(-1), jnp.stack([owner, group])]
    )
    blocks = send_rows(meta, fbank.reshape(load, width), utt, owners)
    received = lax.all_to_all(blocks, "dp", 0, 0, tiled=True)

    grad_out = cotangent.reshape(rows, model)
    grad_t = grad_out.T.reshape(chips, 2, owners, own, rows)
    of_core = lambda side: jnp.swapaxes(at(grad_t, side, 1), 0, 1).reshape(chips * own_rows, rows)
    left = jnp.concatenate([of_core(core), swap(of_core(1 - core))], axis=1)

    norm_in, x0, grad_spaced = front(meta, received, w_sub, gain_in, grad_out, utt, owners)
    norm_in, left = barrier((norm_in, left))
    glu, conv, mean, rstd, swished = forward(meta, norm_in, first_t, taps, gain_mid, rows, utt, owners)

    partial = dot(left, jnp.concatenate([swished, swap(swished)], axis=0)).astype(jnp.bfloat16)
    conv, partial = barrier((conv, partial))
    partial = lax.all_to_all(partial.reshape(owners, chips * own, model), "dp", 0, 0, tiled=True)

    gains = gain_mid.reshape(-1, 1, LANES)
    centered = (conv - mean) * rstd
    normed = centered * gains
    sig = sigmoid(normed)
    slope = gains * (sig * (1.0 + normed * (1.0 - sig)))
    small = backward(grad_spaced, second, slope, centered, rstd, gain_mid, glu, kernel)
    block = (x0.astype(jnp.float32) + dot_t(swished, second)).astype(jnp.bfloat16)

    small = small + swap(small)
    small, partial = scatter_plane(small.reshape(owners, -1, model), owner, partial)
    partial = total_of(partial).reshape(chips, own, model)

    small = small.astype(jnp.bfloat16)
    both = jnp.concatenate([partial, jnp.broadcast_to(small[None], (chips,) + small.shape)], axis=1)
    same_core = [[2 * chip + side for chip in range(chips)] for side in range(2)]
    both = lax.all_to_all(both, "fsdp", 0, 0, tiled=True, axis_index_groups=same_core)
    both = jnp.sum(both.astype(jnp.float32), axis=0).astype(jnp.bfloat16)
    grad_second, grad_taps, grad_gain = outputs(spread(both, "dp"), own, kernel)
    return (block.reshape(1, 1, rows, model), grad_second, grad_taps, grad_gain)


def solution(mesh):
    in_specs = (
        P("dp", "fsdp", None, None),
        P(),
        P(),
        P(),
        P(),
        P(None, "fsdp"),
        P(),
        P(),
        P("fsdp", None),
        P("dp", "fsdp", None, None),
    )
    out_specs = (P("dp", "fsdp", None, None), P("fsdp", None), P(), P())
    return jax.shard_map(body, mesh=mesh, in_specs=in_specs, out_specs=out_specs, check_vma=False)
```
